32 devices in a mesh: groups: 2 (over y), wide: 4 (over z), pair: 2 (over x), cores: 2 (over core).
Axes of the slice: x: 2, y: 2, z: 4, core: 2. Of those that a mesh axis runs over, the one named last changes fastest.
Arguments:
- layer_input: bfloat16 [256, 30, 256], P(('groups', 'wide', 'pair', 'cores')), parts along dimension 0, may hold values from -6 to 6
- mixed_heads: bfloat16 [256, 30, 256], P(('groups', 'wide', 'pair', 'cores')), parts along dimension 0, may hold values from -6 to 6
- cotangents: bfloat16 [256, 4, 30, 256], P(('groups', 'wide', 'pair', 'cores')), parts along dimension 0, may hold values from -0.00012207031 to 0.00012207031
- local_energy: float32 [256], P(('groups', 'wide', 'pair', 'cores')), parts along dimension 0, may hold values from -6 to 6
Outputs:
- update: float32 [2048, 256], P(('groups', 'wide', 'pair', 'cores')), parts along dimension 0
The draws below stay inside these ranges and needn't reach their ends.
There are 2 independent parts, one for each index of `groups`. The reference program is written for one: setup_inputs(seed, part) draws one part's arguments, and reference() takes and returns one part's arrays. A program takes and returns all parts, laid end to end along the dimension named above; each array names one. Nothing has to cross between parts.
All inputs are finite; a program needn't handle non-finite values.
Results may differ from the reference program's by a relative error of at most 0.005.
Values may be sent and summed in bfloat16 or wider, within the bound.
A program may use at most 128 MiB of HBM per device.

```python
import math
import jax
import jax.numpy as jnp
from jax import lax

D = 256
ELEC = 30
WALKERS = 128


def steps_of(key, dims, cuts, smallest, top_value):
    factor_of, own = 1.0, jax.random.fold_in(key, 6)
    for dim, parts in cuts:
        steps = jnp.exp(jax.random.uniform(jax.random.fold_in(own, dim), (parts,), jnp.float32, smallest / len(cuts), top_value / len(cuts)))
        factor_of = factor_of * jnp.repeat(steps, dims[dim] // parts).reshape([-1 if axis == dim else 1 for axis in range(len(dims))])
    return factor_of


def normal_values(stream_key, dims, spread, reach, shards=(), held_as=jnp.bfloat16):
    values = jax.random.normal(stream_key, dims, jnp.float32) * spread
    if len(shards) > 0:
        values = steps_of(stream_key, dims, shards, -0.22, 0.18) * values
    return jnp.clip(values, min=-reach, max=reach).astype(held_as)


def setup_inputs(seed: int = 0, part: int = 0) -> dict:
    keys = jax.random.split(jax.random.key(seed), 5)
    own_keys = jax.random.split(jax.random.fold_in(keys[4], part), 5)
    return {
        "layer_input": normal_values(own_keys[0], (WALKERS, ELEC, D), 1.0, 6.0, ((0, 16),)),
        "mixed_heads": normal_values(own_keys[1], (WALKERS, ELEC, D), 1.0, 6.0, ((0, 16),)),
        "cotangents": normal_values(own_keys[2], (WALKERS, 4, ELEC, D), ((WALKERS / ELEC) ** 0.5 / (4 * D * D)), 0.00012207031, ((0, 16),)),
        "local_energy": normal_values(own_keys[3], (WALKERS,), 1.0, 6.0, ((0, 16),), jnp.float32),
    }


def small_factor(block):
    size = block.shape[0]
    index = jnp.arange(size, dtype=jnp.int32)

    def step(column_id, lower):
        row = lax.dynamic_index_in_dim(lower, column_id, 0, keepdims=False)
        column = lax.dynamic_index_in_dim(block, column_id, 1, keepdims=False) - jnp.dot(lower, row, precision=lax.Precision.HIGHEST)
        pivot = jnp.sqrt(lax.dynamic_index_in_dim(column, column_id, 0, keepdims=False))
        column = jnp.where(index >= column_id, column / pivot, 0.0)
        return jnp.where(index[None, :] == column_id, column[:, None], lower)
    return lax.fori_loop(0, size, step, jnp.zeros_like(block))

def small_inverse(lower):
    size = lower.shape[0]
    index = jnp.arange(size, dtype=jnp.int32)

    def step(row_id, inverse):
        row = lax.dynamic_index_in_dim(lower, row_id, 0, keepdims=False)
        target = (index == row_id).astype(lower.dtype)
        pivot = lax.dynamic_index_in_dim(row, row_id, 0, keepdims=False)
        fresh = (target - jnp.dot(row, inverse, precision=lax.Precision.HIGHEST)) / pivot
        return jnp.where(index[:, None] == row_id, fresh[None, :], inverse)
    return lax.fori_loop(0, size, step, jnp.zeros_like(lower))

def solve_damped(damped, right_side):
    total = damped.shape[0]
    tile = total // 8
    work = damped
    inverses = []
    panels = []
    for block_id in range(8):
        start = block_id * tile
        lower = small_factor(work[start:start + tile, start:start + tile])
        inverse = small_inverse(lower)
        inverses.append(inverse)
        if block_id < 7:
            panel = jnp.dot(work[start + tile:, start:start + tile], inverse.T, precision=lax.Precision.HIGHEST)
            panels.append(panel)
            work = work.at[start + tile:, start + tile:].add(-jnp.dot(panel, panel.T, precision=lax.Precision.HIGHEST))
    forward = []
    for block_id in range(8):
        start = block_id * tile
        residue = right_side[start:start + tile]
        for earlier in range(block_id):
            offset = (block_id - earlier - 1) * tile
            residue = residue - jnp.dot(panels[earlier][offset:offset + tile], forward[earlier], precision=lax.Precision.HIGHEST)
        forward.append(jnp.dot(inverses[block_id], residue, precision=lax.Precision.HIGHEST))
    backward = [None] * 8
    for block_id in range(7, -1, -1):
        residue = forward[block_id]
        if block_id < 7:
            later = jnp.concatenate(backward[block_id + 1:], axis=0)
            residue = residue - jnp.dot(panels[block_id].T, later, precision=lax.Precision.HIGHEST)
        backward[block_id] = jnp.dot(inverses[block_id].T, residue, precision=lax.Precision.HIGHEST)
    return jnp.concatenate(backward, axis=0)

def centered_block(source, cotangent, row_start, inv_root):
    piece = lax.dynamic_slice_in_dim(source, row_start, 8, 2).astype(jnp.float32)
    grads = jnp.einsum('wei,wej->wij', piece, cotangent.astype(jnp.float32))
    stored = lax.optimization_barrier(grads.astype(jnp.bfloat16)).astype(jnp.float32)
    average = lax.optimization_barrier(jnp.mean(stored, axis=0))
    centered = ((stored - average) * inv_root).astype(jnp.bfloat16)
    return centered.reshape(stored.shape[0], stored.shape[1] * stored.shape[2])

def reference(layer_input, mixed_heads, cotangents, local_energy):
    inv_root = 1.0 / math.sqrt(WALKERS)
    starts = jnp.arange(0, D, 8, dtype=jnp.int32)
    sources = (layer_input, layer_input, layer_input, mixed_heads)
    gram = jnp.zeros((WALKERS, WALKERS), jnp.float32)
    for matrix_id in range(4):

        def accumulate(total, row_start, matrix_id=matrix_id):
            block = centered_block(sources[matrix_id], cotangents[:, matrix_id], row_start, inv_root)
            return (total + jnp.dot(block, block.T, preferred_element_type=jnp.float32), None)
        gram, unused = lax.scan(accumulate, gram, starts)
    right_side = (local_energy - jnp.mean(local_energy)) * inv_root
    damped = gram + 0.01 * jnp.trace(gram) / WALKERS * jnp.eye(WALKERS, dtype=jnp.float32)
    coefficients = solve_damped(damped, right_side)
    weights = coefficients.astype(jnp.bfloat16)
    pieces = []
    for matrix_id in range(4):

        def project(row_start, matrix_id=matrix_id):
            block = centered_block(sources[matrix_id], cotangents[:, matrix_id], row_start, inv_root)
            return jnp.dot(weights, block, preferred_element_type=jnp.float32).reshape(8, D)
        pieces.append(lax.map(project, starts).reshape(D, D))
    return jnp.concatenate(pieces, axis=0)
```

```python
import functools
import math

import jax
import jax.numpy as jnp
from jax import lax
from jax.experimental import pallas as pl
from jax.experimental.pallas import tpu as pltpu
from jax.sharding import PartitionSpec as P

MESH = pl.DeviceIdType.MESH
AXES = ("groups", "wide", "pair", "cores")


def solve_damped(damped, right_side):
    lower = jnp.linalg.cholesky(damped)
    forward = jax.scipy.linalg.solve_triangular(lower, right_side, lower=True)
    return jax.scipy.linalg.solve_triangular(lower, forward, lower=True, trans=1)


def gather_kernel(
    nz, nx, rows, elec, inv_root,
    c_ref, st_ref, en_ref, cent_ref, gall_ref,
    cbuf, sz, sx, sbuf, grads, gpart, rbuf, gbuf,
    zs_c, zr_c, zs_s, zr_s, xs_c, xr_c, xs_s, xr_s, cs_c, cr_c, cs_s, cr_s,
    gs, gr, hs, hr,
):
    g, z, x, c = (lax.axis_index(a) for a in AXES)
    nc = 2
    ndev = nz * nx * nc
    sib = 1 - c
    me = (z * nx + x) * nc + c
    used = c_ref.shape[1]
    depth = cbuf.shape[1]
    width = cbuf.shape[2]
    walk = ndev * 8

    def dev(d):
        return (g, d // (nx * nc), (d // nc) % nx, d % nc)

    def clear(o, unused):
        cbuf[o, used:depth, :] = jnp.zeros((depth - used, width), cbuf.dtype)
        return unused
    lax.fori_loop(0, ndev, clear, 0)

    barrier = pltpu.get_barrier_semaphore()

    def greet(k, unused):
        d = lax.rem(me + k, ndev)
        pl.semaphore_signal(barrier, inc=1, device_id=dev(d), device_id_type=MESH)
        return unused
    lax.fori_loop(1, ndev, greet, 0)
    pl.semaphore_wait(barrier, ndev - 1)

    def origin(s, xx, cc):
        return (s * nx + xx) * nc + cc

    def z_copies(zt, src_z, dz):
        m = (4 * zt) // nz
        o = origin(src_z, x, c)
        return (
            pltpu.make_async_remote_copy(
                c_ref.at[m], cbuf.at[o, pl.ds(0, used)], zs_c.at[dz], zr_c.at[src_z],
                device_id=(g, zt, x, c), device_id_type=MESH),
            pltpu.make_async_remote_copy(
                st_ref.at[pl.ds(zt * nx * nc, nx * nc)], sz.at[src_z], zs_s.at[dz], zr_s.at[src_z],
                device_id=(g, zt, x, c), device_id_type=MESH),
        )

    def x_copies(s, xo, xt, dx):
        o = origin(s, xo, c)
        return (
            pltpu.make_async_remote_copy(
                cbuf.at[o, pl.ds(0, used)], cbuf.at[o, pl.ds(0, used)], xs_c.at[dx, s], xr_c.at[xo, s],
                device_id=(g, z, xt, c), device_id_type=MESH),
            pltpu.make_async_remote_copy(
                sz.at[s, pl.ds(xt * nc, nc)], sx.at[xo, s], xs_s.at[dx, s], xr_s.at[xo, s],
                device_id=(g, z, xt, c), device_id_type=MESH),
        )

    def c_copies(s, xo, co, src):
        o = origin(s, xo, co)
        return (
            pltpu.make_async_remote_copy(
                cbuf.at[o, pl.ds(0, used)], cbuf.at[o, pl.ds(0, used)], cs_c.at[xo, s], cr_c.at[xo, s],
                device_id=(g, z, x, sib), device_id_type=MESH),
            pltpu.make_async_remote_copy(
                src, sbuf.at[o], cs_s.at[xo, s], cr_s.at[xo, s],
                device_id=(g, z, x, sib), device_id_type=MESH),
        )

    def z_send(dz, unused):
        for copy in z_copies(lax.rem(z + dz, nz), z, dz):
            copy.start()
        return unused
    lax.fori_loop(1, nz, z_send, 0)

    cbuf[me, 0:used, :] = c_ref[(4 * z) // nz]
    sz[z] = st_ref[pl.ds(z * nx * nc, nx * nc)]

    slot = lax.broadcasted_iota(jnp.int32, (8, depth), 1)
    walker = lax.broadcasted_iota(jnp.int32, (8, depth), 0)
    own = (slot >= walker * elec) & (slot < walker * elec + elec)
    step = min(rows, 16)

    def form(p):
        def part(k, unused):
            base = pl.multiple_of(k * step, step)
            halves = []
            for h in range(nc):
                piece = sbuf[p * nc + h, pl.ds(base, step), :].astype(jnp.float32)
                spread = jnp.where(own[None], piece[:, None, :], 0.0)
                left = spread.reshape(step * 8, depth).astype(jnp.bfloat16)
                out = jnp.dot(left, cbuf[p * nc + h], preferred_element_type=jnp.float32)
                halves.append(out.reshape(step, 8, width))
            both = jnp.concatenate(halves, axis=1).astype(jnp.bfloat16)
            grads[pl.ds(base, step), pl.ds(pl.multiple_of(p * 16, 16), 16), :] = both
            return unused
        lax.fori_loop(0, rows // step, part, 0)

    def pipeline(t, unused):
        @pl.when(t < nz)
        def first():
            s = lax.rem(z + nz - t, nz)

            @pl.when(t > 0)
            def arrived():
                for copy in z_copies(z, s, 0):
                    copy.wait_recv()
            for dx in range(1, nx):
                for copy in x_copies(s, x, lax.rem(x + dx, nx), dx):
                    copy.start()
            for copy in c_copies(s, x, c, sz.at[s, x * nc + sib]):
                copy.start()
            sbuf[origin(s, x, c)] = sz[s, x * nc + c]

        @pl.when((t >= 1) & (t < nz + 1))
        def second():
            s = lax.rem(z + nz - t + 1, nz)
            for dx in range(1, nx):
                xo = lax.rem(x + nx - dx, nx)
                for copy in x_copies(s, xo, x, 0):
                    copy.wait_recv()
                for copy in c_copies(s, xo, c, sx.at[xo, s, sib]):
                    copy.start()
                sbuf[origin(s, xo, c)] = sx[xo, s, c]

        @pl.when(t >= 2)
        def third():
            s = lax.rem(z + nz - t + 2, nz)
            for dx in range(nx):
                xo = lax.rem(x + nx - dx, nx)
                for copy in c_copies(s, xo, sib, sz.at[s, 0]):
                    copy.wait_recv()
                form(s * nx + xo)
        return unused
    lax.fori_loop(0, nz + 2, pipeline, 0)

    gpart[...] = jnp.zeros_like(gpart)
    batch = 4

    def share(k, unused):
        pieces = []
        for j in range(batch):
            stored = grads[k * batch + j].astype(jnp.float32)
            average = jnp.mean(stored, axis=0, keepdims=True)
            piece = ((stored - average) * inv_root).astype(jnp.bfloat16)
            cent_ref[k * batch + j] = piece
            pieces.append(piece)
        flat = jnp.concatenate(pieces, axis=1)
        for r in range(walk // 128):
            add = lax.dot_general(flat[r * 128:(r + 1) * 128], flat, (((1,), (1,)), ((), ())),
                                  preferred_element_type=jnp.float32)
            gpart[r * 16:(r + 1) * 16] += add.reshape(16, 8, walk)
        return unused
    lax.fori_loop(0, rows // batch, share, 0)

    def g_copy(src_d, dst_d, k):
        return pltpu.make_async_remote_copy(
            gpart.at[dst_d], rbuf.at[src_d], gs.at[k], gr.at[src_d], device_id=dev(dst_d), device_id_type=MESH)

    def h_copy(src_d, dst_d, k):
        return pltpu.make_async_remote_copy(
            gbuf.at[src_d], gbuf.at[src_d], hs.at[k], hr.at[src_d], device_id=dev(dst_d), device_id_type=MESH)

    def each(fn):
        def run(k, unused):
            fn(k)
            return unused
        lax.fori_loop(1, ndev, run, 0)

    each(lambda k: g_copy(me, lax.rem(me + k, ndev), k).start())
    rbuf[me] = gpart[me]
    each(lambda k: g_copy(lax.rem(me + k, ndev), me, k).wait_recv())
    gbuf[me, :, 0:walk] = jnp.sum(rbuf[...], axis=0)
    gbuf[me, :, walk:walk + 128] = en_ref[...]
    each(lambda k: h_copy(me, lax.rem(me + k, ndev), k).start())
    each(lambda k: h_copy(lax.rem(me + k, ndev), me, k).wait_recv())
    gall_ref[...] = gbuf[...]

    each(lambda k: g_copy(me, lax.rem(me + k, ndev), k).wait_send())
    each(lambda k: h_copy(me, lax.rem(me + k, ndev), k).wait_send())

    def z_left(dz, unused):
        for copy in z_copies(lax.rem(z + dz, nz), z, dz):
            copy.wait_send()
        return unused
    lax.fori_loop(1, nz, z_left, 0)

    def s_left(s, unused):
        for dx in range(1, nx):
            for copy in x_copies(s, x, lax.rem(x + dx, nx), dx):
                copy.wait_send()
        for xo in range(nx):
            for copy in c_copies(s, xo, c, sz.at[s, 0]):
                copy.wait_send()
        return unused
    lax.fori_loop(0, nz, s_left, 0)


def body(nz, nx, layer_input, mixed_heads, cotangents, local_energy):
    nc = 2
    ndev = nz * nx * nc
    walk_dev, elec, width = layer_input.shape
    walkers = walk_dev * ndev
    inv_root = 1.0 / math.sqrt(walkers)
    rows = 4 * width // ndev
    rows_held = max(rows, 16)
    used = walk_dev * elec
    depth = -(-used // 128) * 128

    def turned(source):
        return jnp.pad(source.reshape(used, width).T, ((0, 0), (0, depth - used)))

    layer = turned(layer_input)
    sources = jnp.concatenate([layer, layer, layer, turned(mixed_heads)], axis=0).reshape(ndev, rows, depth)
    sources = jnp.pad(sources, ((0, 0), (0, rows_held - rows), (0, 0)))
    cots = jnp.swapaxes(cotangents, 0, 1).reshape(4, used, width)
    energy = jnp.broadcast_to(local_energy[:, None], (walk_dev, 128))

    bf, f32 = jnp.bfloat16, jnp.float32
    dma = pltpu.SemaphoreType.DMA
    vmem = pl.BlockSpec(memory_space=pltpu.VMEM)
    centered, everything = pl.pallas_call(
        functools.partial(gather_kernel, nz, nx, rows, elec, inv_root),
        out_shape=(
            jax.ShapeDtypeStruct((rows, walkers, width), bf),
            jax.ShapeDtypeStruct((ndev, walk_dev, walkers + 128), f32),
        ),
        in_specs=[vmem] * 3,
        out_specs=(vmem, vmem),
        scratch_shapes=[
            pltpu.VMEM((ndev, depth, width), bf),
            pltpu.VMEM((nz, nx * nc, rows_held, depth), bf),
            pltpu.VMEM((nx, nz, nc, rows_held, depth), bf),
            pltpu.VMEM((ndev, rows_held, depth), bf),
            pltpu.VMEM((rows, walkers, width), bf),
            pltpu.VMEM((ndev, walk_dev, walkers), f32),
            pltpu.VMEM((ndev, walk_dev, walkers), f32),
            pltpu.VMEM((ndev, walk_dev, walkers + 128), f32),
        ] + [dma((nz,))] * 4 + [dma((nx, nz))] * 8 + [dma((ndev,))] * 4,
        compiler_params=pltpu.CompilerParams(
            collective_id=0, has_side_effects=True, vmem_limit_bytes=56 << 20
        ),
        name="gather_gram",
    )(cots, sources, energy)
    everything = everything.reshape(walkers, walkers + 128)
    gram = everything[:, :walkers]
    energies = everything[:, walkers]
    right_side = (energies - jnp.mean(energies)) * inv_root
    damped = gram + 0.01 * jnp.trace(gram) / walkers * jnp.eye(walkers, dtype=f32)
    weights = solve_damped(damped, right_side).astype(bf)
    return jnp.einsum("w,rwj->rj", weights, centered, preferred_element_type=f32)


def solution(mesh):
    lanes = ("groups", "wide", "pair", "cores")
    placed = (
        P(lanes, None, None),
        P(lanes, None, None),
        P(lanes, None, None, None),
        P(lanes),
    )
    return jax.shard_map(
        functools.partial(body, mesh.shape["wide"], mesh.shape["pair"]),
        mesh=mesh,
        in_specs=placed,
        out_specs=P(lanes, None),
        check_vma=False,
    )
```

```python
import functools
import math

import jax
import jax.numpy as jnp
from jax import lax
from jax.experimental import pallas as pl
from jax.experimental.pallas import tpu as pltpu
from jax.sharding import PartitionSpec as P

MESH = pl.DeviceIdType.MESH
AXES = ("groups", "wide", "pair", "cores")


def solve_damped(damped, right_side):
    lower = jnp.linalg.cholesky(damped)
    forward = jax.scipy.linalg.solve_triangular(lower, right_side, lower=True)
    return jax.scipy.linalg.solve_triangular(lower, forward, lower=True, trans=1)


def gather_kernel(
    nz, nx, rows, elec, inv_root,
    c_ref, st_ref, en_ref, cent_ref, gall_ref,
    cbuf, sz, sx, sbuf, grads, gpart, rbuf, gbuf,
    zs_c, zr_c, zs_s, zr_s, xs_c, xr_c, xs_s, xr_s, cs_c, cr_c, cs_s, cr_s,
    gs, gr, hs, hr,
):
    g, z, x, c = (lax.axis_index(a) for a in AXES)
    nc = 2
    ndev = nz * nx * nc
    sib = 1 - c
    me = (z * nx + x) * nc + c
    used = c_ref.shape[1]
    depth = cbuf.shape[1]
    width = cbuf.shape[2]
    walk = ndev * 8

    def dev(d):
        return (g, d // (nx * nc), (d // nc) % nx, d % nc)

    def clear(o, unused):
        cbuf[o, used:depth, :] = jnp.zeros((depth - used, width), cbuf.dtype)
        return unused
    lax.fori_loop(0, ndev, clear, 0)

    barrier = pltpu.get_barrier_semaphore()

    def greet(k, unused):
        d = lax.rem(me + k, ndev)
        pl.semaphore_signal(barrier, inc=1, device_id=dev(d), device_id_type=MESH)
        return unused
    lax.fori_loop(1, ndev, greet, 0)
    pl.semaphore_wait(barrier, ndev - 1)

    def origin(s, xx, cc):
        return (s * nx + xx) * nc + cc

    def z_copies(zt, src_z, dz):
        m = (4 * zt) // nz
        o = origin(src_z, x, c)
        return (
            pltpu.make_async_remote_copy(
                c_ref.at[m], cbuf.at[o, pl.ds(0, used)], zs_c.at[dz], zr_c.at[src_z],
                device_id=(g, zt, x, c), device_id_type=MESH),
            pltpu.make_async_remote_copy(
                st_ref.at[pl.ds(zt * nx * nc, nx * nc)], sz.at[src_z], zs_s.at[dz], zr_s.at[src_z],
                device_id=(g, zt, x, c), device_id_type=MESH),
        )

    def x_copies(s, xo, xt, dx):
        o = origin(s, xo, c)
        return (
            pltpu.make_async_remote_copy(
                cbuf.at[o, pl.ds(0, used)], cbuf.at[o, pl.ds(0, used)], xs_c.at[dx, s], xr_c.at[xo, s],
                device_id=(g, z, xt, c), device_id_type=MESH),
            pltpu.make_async_remote_copy(
                sz.at[s, pl.ds(xt * nc, nc)], sx.at[xo, s], xs_s.at[dx, s], xr_s.at[xo, s],
                device_id=(g, z, xt, c), device_id_type=MESH),
        )

    def c_copies(s, xo, co, src):
        o = origin(s, xo, co)
        return (
            pltpu.make_async_remote_copy(
                cbuf.at[o, pl.ds(0, used)], cbuf.at[o, pl.ds(0, used)], cs_c.at[xo, s], cr_c.at[xo, s],
                device_id=(g, z, x, sib), device_id_type=MESH),
            pltpu.make_async_remote_copy(
                src, sbuf.at[o], cs_s.at[xo, s], cr_s.at[xo, s],
                device_id=(g, z, x, sib), device_id_type=MESH),
        )

    def z_send(dz, unused):
        for copy in z_copies(lax.rem(z + dz, nz), z, dz):
            copy.start()
        return unused
    lax.fori_loop(1, nz, z_send, 0)

    cbuf[me, 0:used, :] = c_ref[(4 * z) // nz]
    sz[z] = st_ref[pl.ds(z * nx * nc, nx * nc)]

    slot = lax.broadcasted_iota(jnp.int32, (8, depth), 1)
    walker = lax.broadcasted_iota(jnp.int32, (8, depth), 0)
    own = (slot >= walker * elec) & (slot < walker * elec + elec)
    step = min(rows, 16)

    def form(p):
        def part(k, unused):
            base = pl.multiple_of(k * step, step)
            halves = []
            for h in range(nc):
                piece = sbuf[p * nc + h, pl.ds(base, step), :].astype(jnp.float32)
                spread = jnp.where(own[None], piece[:, None, :], 0.0)
                left = spread.reshape(step * 8, depth).astype(jnp.bfloat16)
                out = jnp.dot(left, cbuf[p * nc + h], preferred_element_type=jnp.float32)
                halves.append(out.reshape(step, 8, width))
            both = jnp.concatenate(halves, axis=1).astype(jnp.bfloat16)
            grads[pl.ds(base, step), pl.ds(pl.multiple_of(p * 16, 16), 16), :] = both
            return unused
        lax.fori_loop(0, rows // step, part, 0)

    def pipeline(t, unused):
        @pl.when(t < nz)
        def first():
            s = lax.rem(z + nz - t, nz)

            @pl.when(t > 0)
            def arrived():
                for copy in z_copies(z, s, 0):
                    copy.wait_recv()
            for dx in range(1, nx):
                for copy in x_copies(s, x, lax.rem(x + dx, nx), dx):
                    copy.start()
            for copy in c_copies(s, x, c, sz.at[s, x * nc + sib]):
                copy.start()
            sbuf[origin(s, x, c)] = sz[s, x * nc + c]

        @pl.when((t >= 1) & (t < nz + 1))
        def second():
            s = lax.rem(z + nz - t + 1, nz)
            for dx in range(1, nx):
                xo = lax.rem(x + nx - dx, nx)
                for copy in x_copies(s, xo, x, 0):
                    copy.wait_recv()
                for copy in c_copies(s, xo, c, sx.at[xo, s, sib]):
                    copy.start()
                sbuf[origin(s, xo, c)] = sx[xo, s, c]

        @pl.when(t >= 2)
        def third():
            s = lax.rem(z + nz - t + 2, nz)
            for dx in range(nx):
                xo = lax.rem(x + nx - dx, nx)
                for copy in c_copies(s, xo, sib, sz.at[s, 0]):
                    copy.wait_recv()
                form(s * nx + xo)
        return unused
    lax.fori_loop(0, nz + 2, pipeline, 0)

    gpart[...] = jnp.zeros_like(gpart)
    batch = 4

    def share(k, unused):
        pieces = []
        for j in range(batch):
            stored = grads[k * batch + j].astype(jnp.float32)
            average = jnp.mean(stored, axis=0, keepdims=True)
            piece = ((stored - average) * inv_root).astype(jnp.bfloat16)
            cent_ref[k * batch + j] = piece
            pieces.append(piece)
        flat = jnp.concatenate(pieces, axis=1)
        for r in range(walk // 128):
            add = lax.dot_general(flat[r * 128:(r + 1) * 128], flat, (((1,), (1,)), ((), ())),
                                  preferred_element_type=jnp.float32)
            gpart[r * 16:(r + 1) * 16] += add.reshape(16, 8, walk)
        return unused
    lax.fori_loop(0, rows // batch, share, 0)

    def g_copy(src_d, dst_d, k):
        return pltpu.make_async_remote_copy(
            gpart.at[dst_d], rbuf.at[src_d], gs.at[k], gr.at[src_d], device_id=dev(dst_d), device_id_type=MESH)

    def h_copy(src_d, dst_d, k):
        return pltpu.make_async_remote_copy(
            gbuf.at[src_d], gbuf.at[src_d], hs.at[k], hr.at[src_d], device_id=dev(dst_d), device_id_type=MESH)

    def each(fn):
        def run(k, unused):
            fn(k)
            return unused
        lax.fori_loop(1, ndev, run, 0)

    each(lambda k: g_copy(me, lax.rem(me + k, ndev), k).start())
    rbuf[me] = gpart[me]
    each(lambda k: g_copy(lax.rem(me + k, ndev), me, k).wait_recv())
    gbuf[me, :, 0:walk] = jnp.sum(rbuf[...], axis=0)
    gbuf[me, :, walk:walk + 128] = en_ref[...]
    each(lambda k: h_copy(me, lax.rem(me + k, ndev), k).start())
    each(lambda k: h_copy(lax.rem(me + k, ndev), me, k).wait_recv())
    gall_ref[...] = gbuf[...]

    each(lambda k: g_copy(me, lax.rem(me + k, ndev), k).wait_send())
    each(lambda k: h_copy(me, lax.rem(me + k, ndev), k).wait_send())

    def z_left(dz, unused):
        for copy in z_copies(lax.rem(z + dz, nz), z, dz):
            copy.wait_send()
        return unused
    lax.fori_loop(1, nz, z_left, 0)

    def s_left(s, unused):
        for dx in range(1, nx):
            for copy in x_copies(s, x, lax.rem(x + dx, nx), dx):
                copy.wait_send()
        for xo in range(nx):
            for copy in c_copies(s, xo, c, sz.at[s, 0]):
                copy.wait_send()
        return unused
    lax.fori_loop(0, nz, s_left, 0)


def solve_kernel(inv_root, all_ref, cent_ref, out_ref):
    tiles, size, wide = all_ref.shape
    walkers = tiles * size
    lane = lax.broadcasted_iota(jnp.int32, (size, walkers), 1)
    sub = lax.broadcasted_iota(jnp.int32, (size, walkers), 0)
    a = [all_ref[i, :, 0:walkers] for i in range(tiles)]
    e = [all_ref[i, :, walkers:wide] for i in range(tiles)]
    diagonal = [lane == sub + size * i for i in range(tiles)]
    picked = jnp.where(diagonal[0], a[0], 0.0)
    total = e[0]
    for i in range(1, tiles):
        picked = picked + jnp.where(diagonal[i], a[i], 0.0)
        total = total + e[i]
    shift = 0.01 * jnp.sum(jnp.sum(picked, axis=0, keepdims=True), axis=1, keepdims=True) / walkers
    average = jnp.sum(total, axis=0, keepdims=True) / walkers
    y = [(e[i] - average) * inv_root for i in range(tiles)]
    a = [a[i] + jnp.where(diagonal[i], shift, 0.0) for i in range(tiles)]

    for k in range(tiles):
        spread = [
            [jnp.broadcast_to(a[i][:, size * k + j:size * k + j + 1], (size, walkers)) for j in range(size)]
            for i in range(tiles)
        ]
        c = list(spread[k])
        row, right = a[k], y[k]
        scale = jnp.zeros((size, walkers), jnp.float32)
        for j in range(size):
            inverse = 1.0 / c[j][j:j + 1, :]
            factor = jnp.where(sub == j, 0.0, c[j]) * inverse
            for l in range(j + 1, size):
                c[l] = c[l] - factor * c[l][j:j + 1, :]
            row = row - factor * row[j:j + 1, :]
            right = right - factor * right[j:j + 1, :]
            scale = jnp.where(sub == j, inverse, scale)
        row, right = row * scale, right * scale
        a[k], y[k] = row, right
        order = [(k + 1 + i) % tiles for i in range(tiles - 1)]
        for i in order:
            for j in range(size):
                if k + 1 < tiles:
                    a[i] = a[i] - spread[i][j] * row[j:j + 1, :]
                y[i] = y[i] - spread[i][j] * right[j:j + 1, :]

    weights = [v.astype(jnp.bfloat16).astype(jnp.float32) for v in y]
    column = jnp.concatenate(weights, axis=0)
    rows, _, width = cent_ref.shape
    column = jnp.concatenate([column] * (width // walkers), axis=1)

    def project(r, unused):
        base = pl.multiple_of(r * 8, 8)
        parts = [
            jnp.sum(cent_ref[base + q].astype(jnp.float32) * column, axis=0, keepdims=True) for q in range(8)
        ]
        out_ref[pl.ds(base, 8), :] = jnp.concatenate(parts, axis=0)
        return unused
    lax.fori_loop(0, rows // 8, project, 0)


def body(nz, nx, layer_input, mixed_heads, cotangents, local_energy):
    nc = 2
    ndev = nz * nx * nc
    walk_dev, elec, width = layer_input.shape
    walkers = walk_dev * ndev
    inv_root = 1.0 / math.sqrt(walkers)
    rows = 4 * width // ndev
    rows_held = max(rows, 16)
    used = walk_dev * elec
    depth = -(-used // 128) * 128

    def turned(source):
        return jnp.pad(source.reshape(used, width).T, ((0, 0), (0, depth - used)))

    layer = turned(layer_input)
    sources = jnp.concatenate([layer, layer, layer, turned(mixed_heads)], axis=0).reshape(ndev, rows, depth)
    sources = jnp.pad(sources, ((0, 0), (0, rows_held - rows), (0, 0)))
    cots = jnp.swapaxes(cotangents, 0, 1).reshape(4, used, width)
    energy = jnp.broadcast_to(local_energy[:, None], (walk_dev, 128))

    bf, f32 = jnp.bfloat16, jnp.float32
    dma = pltpu.SemaphoreType.DMA
    vmem = pl.BlockSpec(memory_space=pltpu.VMEM)
    centered, everything = pl.pallas_call(
        functools.partial(gather_kernel, nz, nx, rows, elec, inv_root),
        out_shape=(
            jax.ShapeDtypeStruct((rows, walkers, width), bf),
            jax.ShapeDtypeStruct((ndev, walk_dev, walkers + 128), f32),
        ),
        in_specs=[vmem] * 3,
        out_specs=(vmem, vmem),
        scratch_shapes=[
            pltpu.VMEM((ndev, depth, width), bf),
            pltpu.VMEM((nz, nx * nc, rows_held, depth), bf),
            pltpu.VMEM((nx, nz, nc, rows_held, depth), bf),
            pltpu.VMEM((ndev, rows_held, depth), bf),
            pltpu.VMEM((rows, walkers, width), bf),
            pltpu.VMEM((ndev, walk_dev, walkers), f32),
            pltpu.VMEM((ndev, walk_dev, walkers), f32),
            pltpu.VMEM((ndev, walk_dev, walkers + 128), f32),
        ] + [dma((nz,))] * 4 + [dma((nx, nz))] * 8 + [dma((ndev,))] * 4,
        compiler_params=pltpu.CompilerParams(
            collective_id=0, has_side_effects=True, vmem_limit_bytes=56 << 20
        ),
        name="gather_gram",
    )(cots, sources, energy)
    if walkers == 128:
        return pl.pallas_call(
            functools.partial(solve_kernel, inv_root),
            out_shape=jax.ShapeDtypeStruct((rows, width), f32),
            in_specs=[vmem] * 2,
            out_specs=vmem,
            compiler_params=pltpu.CompilerParams(vmem_limit_bytes=32 << 20),
            name="solve_project",
        )(everything, centered)
    everything = everything.reshape(walkers, walkers + 128)
    gram = everything[:, :walkers]
    energies = everything[:, walkers]
    right_side = (energies - jnp.mean(energies)) * inv_root
    damped = gram + 0.01 * jnp.trace(gram) / walkers * jnp.eye(walkers, dtype=f32)
    weights = solve_damped(damped, right_side).astype(bf)
    return jnp.einsum("w,rwj->rj", weights, centered, preferred_element_type=f32)


def solution(mesh):
    lanes = ("groups", "wide", "pair", "cores")
    placed = (
        P(lanes, None, None),
        P(lanes, None, None),
        P(lanes, None, None, None),
        P(lanes),
    )
    return jax.shard_map(
        functools.partial(body, mesh.shape["wide"], mesh.shape["pair"]),
        mesh=mesh,
        in_specs=placed,
        out_specs=P(lanes, None),
        check_vma=False,
    )
```

```python
import functools
import math

import jax
import jax.numpy as jnp
from jax import lax
from jax.experimental import pallas as pl
from jax.experimental.pallas import tpu as pltpu
from jax.sharding import PartitionSpec as P

MESH = pl.DeviceIdType.MESH
AXES = ("groups", "wide", "pair", "cores")


def solve_damped(damped, right_side):
    lower = jnp.linalg.cholesky(damped)
    forward = jax.scipy.linalg.solve_triangular(lower, right_side, lower=True)
    return jax.scipy.linalg.solve_triangular(lower, forward, lower=True, trans=1)


def gather_kernel(
    nz, nx, rows, inv_root,
    layer_ref, heads_ref, cot_ref, en_ref, cent_ref, gall_ref,
    c_ref, st_ref, turn, cbuf, sz, sx, sbuf, grads, gpart, rbuf, gbuf,
    zs_c, zr_c, zs_s, zr_s, xs_c, xr_c, xs_s, xr_s, cs_c, cr_c, cs_s, cr_s,
    gs, gr, hs, hr,
):
    g, z, x, c = (lax.axis_index(a) for a in AXES)
    nc = 2
    ndev = nz * nx * nc
    sib = 1 - c
    me = (z * nx + x) * nc + c
    depth = cbuf.shape[1]
    width = cbuf.shape[2]
    walk = ndev * 8

    def dev(d):
        return (g, d // (nx * nc), (d // nc) % nx, d % nc)

    barrier = pltpu.get_barrier_semaphore()

    def greet(k, unused):
        d = lax.rem(me + k, ndev)
        pl.semaphore_signal(barrier, inc=1, device_id=dev(d), device_id_type=MESH)
        return unused
    lax.fori_loop(1, ndev, greet, 0)

    elec = layer_ref.shape[1]
    slot_rows = depth // 8
    c_ref[...] = jnp.zeros_like(c_ref)
    for w in range(8):
        for m in range(4):
            c_ref[m, w * slot_rows:w * slot_rows + elec, :] = cot_ref[w, m]
    turn[...] = jnp.zeros_like(turn)
    slabs = width // rows
    for source, first_slab, times in ((layer_ref, 0, 3), (heads_ref, 3 * slabs, 1)):
        for w in range(8):
            turn[w * slot_rows:w * slot_rows + elec, :] = source[w].astype(jnp.float32)
        turned = turn[...].T.astype(jnp.bfloat16).reshape(slabs, rows, depth)
        for again in range(times):
            at = first_slab + again * slabs
            st_ref[at:at + slabs, 0:rows, :] = turned
    if st_ref.shape[1] > rows:
        st_ref[:, rows:, :] = jnp.zeros((ndev, st_ref.shape[1] - rows, depth), jnp.bfloat16)
    pl.semaphore_wait(barrier, ndev - 1)

    def origin(s, xx, cc):
        return (s * nx + xx) * nc + cc

    def z_copies(zt, src_z, dz):
        m = (4 * zt) // nz
        o = origin(src_z, x, c)
        return (
            pltpu.make_async_remote_copy(
                c_ref.at[m], cbuf.at[o], zs_c.at[dz], zr_c.at[src_z],
                device_id=(g, zt, x, c), device_id_type=MESH),
            pltpu.make_async_remote_copy(
                st_ref.at[pl.ds(zt * nx * nc, nx * nc)], sz.at[src_z], zs_s.at[dz], zr_s.at[src_z],
                device_id=(g, zt, x, c), device_id_type=MESH),
        )

    def x_copies(s, xo, xt, dx):
        o = origin(s, xo, c)
        return (
            pltpu.make_async_remote_copy(
                cbuf.at[o], cbuf.at[o], xs_c.at[dx, s], xr_c.at[xo, s],
                device_id=(g, z, xt, c), device_id_type=MESH),
            pltpu.make_async_remote_copy(
                sz.at[s, pl.ds(xt * nc, nc)], sx.at[xo, s], xs_s.at[dx, s], xr_s.at[xo, s],
                device_id=(g, z, xt, c), device_id_type=MESH),
        )

    def c_copies(s, xo, co, src):
        o = origin(s, xo, co)
        return (
            pltpu.make_async_remote_copy(
                cbuf.at[o], cbuf.at[o], cs_c.at[xo, s], cr_c.at[xo, s],
                device_id=(g, z, x, sib), device_id_type=MESH),
            pltpu.make_async_remote_copy(
                src, sbuf.at[o], cs_s.at[xo, s], cr_s.at[xo, s],
                device_id=(g, z, x, sib), device_id_type=MESH),
        )

    half = nz // 2

    def offset(t):
        away = jnp.where(lax.rem(t, 2) == 0, half - t // 2, half + t // 2)
        return jnp.where(t == 0, 0, away)

    def z_round(t):
        return z_copies(lax.rem(z + offset(t), nz), z, t)

    def z_from(t):
        return lax.rem(z + nz - offset(t), nz)

    for copy in z_round(1):
        copy.start()

    cbuf[me] = c_ref[(4 * z) // nz]
    sz[z] = st_ref[pl.ds(z * nx * nc, nx * nc)]

    slot = lax.broadcasted_iota(jnp.int32, (8, depth), 1)
    walker = lax.broadcasted_iota(jnp.int32, (8, depth), 0)
    own = (slot >= walker * slot_rows) & (slot < (walker + 1) * slot_rows)
    step = min(rows, 16)

    def form(p):
        def part(k, unused):
            base = pl.multiple_of(k * step, step)
            halves = []
            for h in range(nc):
                piece = sbuf[p * nc + h, pl.ds(base, step), :].astype(jnp.float32)
                spread = jnp.where(own[None], piece[:, None, :], 0.0)
                left = spread.reshape(step * 8, depth).astype(jnp.bfloat16)
                out = jnp.dot(left, cbuf[p * nc + h], preferred_element_type=jnp.float32)
                halves.append(out.reshape(step, 8, width))
            both = jnp.concatenate(halves, axis=1).astype(jnp.bfloat16)
            grads[pl.ds(base, step), pl.ds(pl.multiple_of(p * 16, 16), 16), :] = both
            return unused
        lax.fori_loop(0, rows // step, part, 0)

    def pipeline(t, unused):
        @pl.when(t < nz)
        def first():
            s = z_from(t)

            @pl.when((t > 0) & (t < nz - 1))
            def onward():
                for copy, later in zip(z_round(t), z_round(t + 1)):
                    copy.wait_send()
                    later.start()

            @pl.when(t > 0)
            def arrived():
                for copy in z_copies(z, s, 0):
                    copy.wait_recv()
            for dx in range(1, nx):
                for copy in x_copies(s, x, lax.rem(x + dx, nx), dx):
                    copy.start()
            for copy in c_copies(s, x, c, sz.at[s, x * nc + sib]):
                copy.start()
            sbuf[origin(s, x, c)] = sz[s, x * nc + c]

        @pl.when((t >= 1) & (t < nz + 1))
        def second():
            s = z_from(t - 1)
            for dx in range(1, nx):
                xo = lax.rem(x + nx - dx, nx)
                for copy in x_copies(s, xo, x, 0):
                    copy.wait_recv()
                for copy in c_copies(s, xo, c, sx.at[xo, s, sib]):
                    copy.start()
                sbuf[origin(s, xo, c)] = sx[xo, s, c]

        @pl.when(t >= 2)
        def third():
            s = z_from(t - 2)
            for dx in range(nx):
                xo = lax.rem(x + nx - dx, nx)
                for copy in c_copies(s, xo, sib, sz.at[s, 0]):
                    copy.wait_recv()
                form(s * nx + xo)
        return unused
    lax.fori_loop(0, nz + 2, pipeline, 0)

    gpart[...] = jnp.zeros_like(gpart)
    batch = 4

    def share(k, unused):
        pieces = []
        for j in range(batch):
            stored = grads[k * batch + j].astype(jnp.float32)
            average = jnp.mean(stored, axis=0, keepdims=True)
            piece = ((stored - average) * inv_root).astype(jnp.bfloat16)
            cent_ref[k * batch + j] = piece
            pieces.append(piece)
        flat = jnp.concatenate(pieces, axis=1)
        for r in range(walk // 128):
            add = lax.dot_general(flat[r * 128:(r + 1) * 128], flat, (((1,), (1,)), ((), ())),
                                  preferred_element_type=jnp.float32)
            gpart[r * 16:(r + 1) * 16] += add.reshape(16, 8, walk)
        return unused
    lax.fori_loop(0, rows // batch, share, 0, unroll=2)

    def g_copy(src_d, dst_d, k):
        return pltpu.make_async_remote_copy(
            gpart.at[dst_d], rbuf.at[src_d], gs.at[k], gr.at[src_d], device_id=dev(dst_d), device_id_type=MESH)

    def h_copy(src_d, dst_d, k):
        return pltpu.make_async_remote_copy(
            gbuf.at[src_d], gbuf.at[src_d], hs.at[k], hr.at[src_d], device_id=dev(dst_d), device_id_type=MESH)

    def each(fn):
        def run(k, unused):
            fn(k)
            return unused
        lax.fori_loop(1, ndev, run, 0)

    each(lambda k: g_copy(me, lax.rem(me + k, ndev), k).start())
    rbuf[me] = gpart[me]
    each(lambda k: g_copy(lax.rem(me + k, ndev), me, k).wait_recv())
    gbuf[me, :, 0:walk] = jnp.sum(rbuf[...], axis=0)
    energy = jnp.zeros((8, 128), jnp.float32)
    place = lax.broadcasted_iota(jnp.int32, (8, 128), 0)
    for w in range(8):
        energy = jnp.where(place == w, en_ref[w], energy)
    gbuf[me, :, walk:walk + 128] = energy
    each(lambda k: h_copy(me, lax.rem(me + k, ndev), k).start())
    each(lambda k: h_copy(lax.rem(me + k, ndev), me, k).wait_recv())
    gall_ref[...] = gbuf[...]

    each(lambda k: g_copy(me, lax.rem(me + k, ndev), k).wait_send())
    each(lambda k: h_copy(me, lax.rem(me + k, ndev), k).wait_send())

    for copy in z_round(nz - 1):
        copy.wait_send()

    def s_left(s, unused):
        for dx in range(1, nx):
            for copy in x_copies(s, x, lax.rem(x + dx, nx), dx):
                copy.wait_send()
        for xo in range(nx):
            for copy in c_copies(s, xo, c, sz.at[s, 0]):
                copy.wait_send()
        return unused
    lax.fori_loop(0, nz, s_left, 0)


def solve_kernel(inv_root, all_ref, cent_ref, out_ref):
    tiles, size, wide = all_ref.shape
    walkers = tiles * size
    lane = lax.broadcasted_iota(jnp.int32, (size, walkers), 1)
    sub = lax.broadcasted_iota(jnp.int32, (size, walkers), 0)
    a = [all_ref[i, :, 0:walkers] for i in range(tiles)]
    e = [all_ref[i, :, walkers:wide] for i in range(tiles)]
    diagonal = [lane == sub + size * i for i in range(tiles)]
    picked = jnp.where(diagonal[0], a[0], 0.0)
    total = e[0]
    for i in range(1, tiles):
        picked = picked + jnp.where(diagonal[i], a[i], 0.0)
        total = total + e[i]
    shift = 0.01 * jnp.sum(jnp.sum(picked, axis=0, keepdims=True), axis=1, keepdims=True) / walkers
    average = jnp.sum(total, axis=0, keepdims=True) / walkers
    y = [(e[i] - average) * inv_root for i in range(tiles)]
    a = [a[i] + jnp.where(diagonal[i], shift, 0.0) for i in range(tiles)]

    for k in range(tiles):
        spread = [
            [jnp.broadcast_to(a[i][:, size * k + j:size * k + j + 1], (size, walkers)) for j in range(size)]
            for i in range(tiles)
        ]
        c = list(spread[k])
        row, right = a[k], y[k]
        scale = jnp.zeros((size, walkers), jnp.float32)
        for j in range(size):
            inverse = 1.0 / c[j][j:j + 1, :]
            factor = jnp.where(sub == j, 0.0, c[j]) * inverse
            for l in range(j + 1, size):
                c[l] = c[l] - factor * c[l][j:j + 1, :]
            row = row - factor * row[j:j + 1, :]
            right = right - factor * right[j:j + 1, :]
            scale = jnp.where(sub == j, inverse, scale)
        row, right = row * scale, right * scale
        a[k], y[k] = row, right
        order = [(k + 1 + i) % tiles for i in range(tiles - 1)]
        for i in order:
            for j in range(size):
                if k + 1 < tiles:
                    a[i] = a[i] - spread[i][j] * row[j:j + 1, :]
                y[i] = y[i] - spread[i][j] * right[j:j + 1, :]

    weights = [v.astype(jnp.bfloat16).astype(jnp.float32) for v in y]
    column = jnp.concatenate(weights, axis=0)
    rows, _, width = cent_ref.shape
    column = jnp.concatenate([column] * (width // walkers), axis=1)

    def project(r, unused):
        base = pl.multiple_of(r * 8, 8)
        parts = [
            jnp.sum(cent_ref[base + q].astype(jnp.float32) * column, axis=0, keepdims=True) for q in range(8)
        ]
        out_ref[pl.ds(base, 8), :] = jnp.concatenate(parts, axis=0)
        return unused
    lax.fori_loop(0, rows // 8, project, 0)


def body(nz, nx, layer_input, mixed_heads, cotangents, local_energy):
    nc = 2
    ndev = nz * nx * nc
    walk_dev, elec, width = layer_input.shape
    walkers = walk_dev * ndev
    inv_root = 1.0 / math.sqrt(walkers)
    rows = 4 * width // ndev
    rows_held = max(rows, 16)
    depth = walk_dev * (-(-elec // 16) * 16)

    bf, f32 = jnp.bfloat16, jnp.float32
    dma = pltpu.SemaphoreType.DMA
    vmem = pl.BlockSpec(memory_space=pltpu.VMEM)
    centered, everything = pl.pallas_call(
        functools.partial(gather_kernel, nz, nx, rows, inv_root),
        out_shape=(
            jax.ShapeDtypeStruct((rows, walkers, width), bf),
            jax.ShapeDtypeStruct((ndev, walk_dev, walkers + 128), f32),
        ),
        in_specs=[vmem] * 3 + [pl.BlockSpec(memory_space=pltpu.SMEM)],
        out_specs=(vmem, vmem),
        scratch_shapes=[
            pltpu.VMEM((4, depth, width), bf),
            pltpu.VMEM((ndev, rows_held, depth), bf),
            pltpu.VMEM((depth, width), f32),
            pltpu.VMEM((ndev, depth, width), bf),
            pltpu.VMEM((nz, nx * nc, rows_held, depth), bf),
            pltpu.VMEM((nx, nz, nc, rows_held, depth), bf),
            pltpu.VMEM((ndev, rows_held, depth), bf),
            pltpu.VMEM((rows, walkers, width), bf),
            pltpu.VMEM((ndev, walk_dev, walkers), f32),
            pltpu.VMEM((ndev, walk_dev, walkers), f32),
            pltpu.VMEM((ndev, walk_dev, walkers + 128), f32),
        ] + [dma((nz,))] * 4 + [dma((nx, nz))] * 8 + [dma((ndev,))] * 4,
        compiler_params=pltpu.CompilerParams(
            collective_id=0, has_side_effects=True, vmem_limit_bytes=56 << 20
        ),
        name="gather_gram",
    )(layer_input, mixed_heads, cotangents, local_energy)
    if walkers == 128:
        return pl.pallas_call(
            functools.partial(solve_kernel, inv_root),
            out_shape=jax.ShapeDtypeStruct((rows, width), f32),
            in_specs=[vmem] * 2,
            out_specs=vmem,
            compiler_params=pltpu.CompilerParams(vmem_limit_bytes=32 << 20),
            name="solve_project",
        )(everything, centered)
    everything = everything.reshape(walkers, walkers + 128)
    gram = everything[:, :walkers]
    energies = everything[:, walkers]
    right_side = (energies - jnp.mean(energies)) * inv_root
    damped = gram + 0.01 * jnp.trace(gram) / walkers * jnp.eye(walkers, dtype=f32)
    weights = solve_damped(damped, right_side).astype(bf)
    return jnp.einsum("w,rwj->rj", weights, centered, preferred_element_type=f32)


def solution(mesh):
    lanes = ("groups", "wide", "pair", "cores")
    placed = (
        P(lanes, None, None),
        P(lanes, None, None),
        P(lanes, None, None, None),
        P(lanes),
    )
    return jax.shard_map(
        functools.partial(body, mesh.shape["wide"], mesh.shape["pair"]),
        mesh=mesh,
        in_specs=placed,
        out_specs=P(lanes, None),
        check_vma=False,
    )
```

```python
import functools
import math

import jax
import jax.numpy as jnp
from jax import lax
from jax.experimental import pallas as pl
from jax.experimental.pallas import tpu as pltpu
from jax.sharding import PartitionSpec as P

MESH = pl.DeviceIdType.MESH
AXES = ("groups", "wide", "pair", "cores")


def solve_damped(damped, right_side):
    lower = jnp.linalg.cholesky(damped)
    forward = jax.scipy.linalg.solve_triangular(lower, right_side, lower=True)
    return jax.scipy.linalg.solve_triangular(lower, forward, lower=True, trans=1)


def gather_kernel(
    nz, nx, rows, inv_root,
    layer_ref, heads_ref, c_ref, en_ref, cent_ref, gall_ref,
    st_ref, cbuf, sz, sx, sbuf, grads, gpart, rbuf, gbuf,
    zs_c, zr_c, zs_s, zr_s, xs_c, xr_c, xs_s, xr_s, cs_c, cr_c, cs_s, cr_s,
    gs, gr, hs, hr,
):
    g, z, x, c = (lax.axis_index(a) for a in AXES)
    nc = 2
    ndev = nz * nx * nc
    sib = 1 - c
    me = (z * nx + x) * nc + c
    depth = cbuf.shape[1]
    width = cbuf.shape[2]
    walk = ndev * 8

    def dev(d):
        return (g, d // (nx * nc), (d // nc) % nx, d % nc)

    barrier = pltpu.get_barrier_semaphore()

    def greet(k, unused):
        d = lax.rem(me + k, ndev)
        pl.semaphore_signal(barrier, inc=1, device_id=dev(d), device_id_type=MESH)
        return unused
    lax.fori_loop(1, ndev, greet, 0, unroll=ndev <= 16)

    used = c_ref.shape[1]

    def clear(o, unused):
        cbuf[o, used:depth, :] = jnp.zeros((depth - used, width), cbuf.dtype)
        return unused
    lax.fori_loop(0, ndev, clear, 0)
    st_ref[...] = jnp.zeros_like(st_ref)
    slabs = width // rows
    for source, first_slab, times in ((layer_ref, 0, 3), (heads_ref, 3 * slabs, 1)):
        turned = source[...].astype(jnp.float32).T.astype(jnp.bfloat16).reshape(slabs, rows, used)
        for again in range(times):
            at = first_slab + again * slabs
            st_ref[at:at + slabs, 0:rows, 0:used] = turned
    pl.semaphore_wait(barrier, ndev - 1)

    def origin(s, xx, cc):
        return (s * nx + xx) * nc + cc

    def z_copies(zt, src_z, dz):
        m = (4 * zt) // nz
        o = origin(src_z, x, c)
        copies = [pltpu.make_async_remote_copy(
            c_ref.at[m], cbuf.at[o, pl.ds(0, used)], zs_c.at[dz], zr_c.at[src_z],
            device_id=(g, zt, x, c), device_id_type=MESH)]
        for dx in range(1, nx + 1):
            xt = lax.rem(x + dx, nx)
            copies.append(pltpu.make_async_remote_copy(
                st_ref.at[pl.ds((zt * nx + xt) * nc, nc)], sz.at[src_z, pl.ds(xt * nc, nc)],
                zs_s.at[dx - 1, dz], zr_s.at[dx - 1, src_z],
                device_id=(g, zt, x, c), device_id_type=MESH))
        return copies

    def x_copies(s, xo, xt, dx):
        o = origin(s, xo, c)
        return (
            pltpu.make_async_remote_copy(
                cbuf.at[o, pl.ds(0, used)], cbuf.at[o, pl.ds(0, used)], xs_c.at[dx, s], xr_c.at[xo, s],
                device_id=(g, z, xt, c), device_id_type=MESH),
            pltpu.make_async_remote_copy(
                sz.at[s, pl.ds(xt * nc, nc)], sx.at[xo, s], xs_s.at[dx, s], xr_s.at[xo, s],
                device_id=(g, z, xt, c), device_id_type=MESH),
        )

    def c_copies(s, xo, co, src):
        o = origin(s, xo, co)
        return (
            pltpu.make_async_remote_copy(
                cbuf.at[o, pl.ds(0, used)], cbuf.at[o, pl.ds(0, used)], cs_c.at[xo, s], cr_c.at[xo, s],
                device_id=(g, z, x, sib), device_id_type=MESH),
            pltpu.make_async_remote_copy(
                src, sbuf.at[o], cs_s.at[xo, s], cr_s.at[xo, s],
                device_id=(g, z, x, sib), device_id_type=MESH),
        )

    half = nz // 2

    def offset(t):
        away = jnp.where(lax.rem(t, 2) == 0, half - t // 2, half + t // 2)
        return jnp.where(t == 0, 0, away)

    def z_round(t):
        return z_copies(lax.rem(z + offset(t), nz), z, t)

    def z_from(t):
        return lax.rem(z + nz - offset(t), nz)

    for copy in z_round(1) + z_round(2)[:1]:
        copy.start()

    cbuf[me, 0:used, :] = c_ref[(4 * z) // nz]
    sz[z] = st_ref[pl.ds(z * nx * nc, nx * nc)]

    slot = lax.broadcasted_iota(jnp.int32, (8, depth), 1)
    walker = lax.broadcasted_iota(jnp.int32, (8, depth), 0)
    own = lax.rem(slot, 8) == walker
    step = min(rows, 16)

    def form(p):
        def part(k, unused):
            base = pl.multiple_of(k * step, step)
            halves = []
            for h in range(nc):
                piece = sbuf[p * nc + h, pl.ds(base, step), :].astype(jnp.float32)
                spread = jnp.where(own[None], piece[:, None, :], 0.0)
                left = spread.reshape(step * 8, depth).astype(jnp.bfloat16)
                out = jnp.dot(left, cbuf[p * nc + h], preferred_element_type=jnp.float32)
                halves.append(out.reshape(step, 8, width))
            both = jnp.concatenate(halves, axis=1).astype(jnp.bfloat16)
            grads[pl.ds(base, step), pl.ds(pl.multiple_of(p * 16, 16), 16), :] = both
            return unused
        lax.fori_loop(0, rows // step, part, 0)

    def pipeline(t, unused):
        @pl.when(t < nz)
        def first():
            s = z_from(t)

            def land(j):
                @pl.when(t > 0)
                def arrived():
                    z_round(t)[j].wait_send()
                    ahead = 1 if j < nx else 2

                    @pl.when(t + ahead < nz)
                    def onward():
                        z_round(t + ahead)[(j + 1) % (nx + 1)].start()
                    z_copies(z, s, 0)[j].wait_recv()

            to_sib = c_copies(s, x, c, sz.at[s, x * nc + sib])
            land(0)
            for dx in range(1, nx):
                x_copies(s, x, lax.rem(x + dx, nx), dx)[0].start()
            to_sib[0].start()
            for dx in range(1, nx):
                land(dx)
                x_copies(s, x, lax.rem(x + dx, nx), dx)[1].start()
            land(nx)
            to_sib[1].start()
            sbuf[origin(s, x, c)] = sz[s, x * nc + c]

        @pl.when((t >= 1) & (t < nz + 1))
        def second():
            s = z_from(t - 1)
            for dx in range(1, nx):
                xo = lax.rem(x + nx - dx, nx)
                for copy, onward in zip(x_copies(s, xo, x, 0), c_copies(s, xo, c, sx.at[xo, s, sib])):
                    copy.wait_recv()
                    onward.start()
                sbuf[origin(s, xo, c)] = sx[xo, s, c]

        @pl.when(t >= 2)
        def third():
            s = z_from(t - 2)
            for dx in range(nx):
                xo = lax.rem(x + nx - dx, nx)
                for copy in c_copies(s, xo, sib, sz.at[s, 0]):
                    copy.wait_recv()
                form(s * nx + xo)
        return unused
    lax.fori_loop(0, nz + 2, pipeline, 0)

    gpart[...] = jnp.zeros_like(gpart)
    batch = 4

    def share(k, unused):
        pieces = []
        for j in range(batch):
            stored = grads[k * batch + j].astype(jnp.float32)
            average = jnp.mean(stored, axis=0, keepdims=True)
            piece = ((stored - average) * inv_root).astype(jnp.bfloat16)
            cent_ref[k * batch + j] = piece
            pieces.append(piece)
        flat = jnp.concatenate(pieces, axis=1)
        for r in range(walk // 128):
            add = lax.dot_general(flat[r * 128:(r + 1) * 128], flat, (((1,), (1,)), ((), ())),
                                  preferred_element_type=jnp.float32)
            gpart[r * 16:(r + 1) * 16] += add.reshape(16, 8, walk)
        return unused
    lax.fori_loop(0, rows // batch, share, 0, unroll=2)

    def g_copy(src_d, dst_d, k):
        return pltpu.make_async_remote_copy(
            gpart.at[dst_d], rbuf.at[src_d], gs.at[k], gr.at[src_d], device_id=dev(dst_d), device_id_type=MESH)

    def h_copy(src_d, dst_d, k):
        return pltpu.make_async_remote_copy(
            gbuf.at[src_d], gbuf.at[src_d], hs.at[k], hr.at[src_d], device_id=dev(dst_d), device_id_type=MESH)

    def each(fn):
        def run(k, unused):
            fn(k)
            return unused
        lax.fori_loop(1, ndev, run, 0, unroll=ndev <= 16)

    each(lambda k: g_copy(me, lax.rem(me + k, ndev), k).start())
    rbuf[me] = gpart[me]
    each(lambda k: g_copy(lax.rem(me + k, ndev), me, k).wait_recv())
    gbuf[me, :, 0:walk] = jnp.sum(rbuf[...], axis=0)
    energy = jnp.zeros((8, 128), jnp.float32)
    place = lax.broadcasted_iota(jnp.int32, (8, 128), 0)
    for w in range(8):
        energy = jnp.where(place == w, en_ref[w], energy)
    gbuf[me, :, walk:walk + 128] = energy
    each(lambda k: h_copy(me, lax.rem(me + k, ndev), k).start())
    each(lambda k: h_copy(lax.rem(me + k, ndev), me, k).wait_recv())
    gall_ref[...] = gbuf[...]

    each(lambda k: g_copy(me, lax.rem(me + k, ndev), k).wait_send())
    each(lambda k: h_copy(me, lax.rem(me + k, ndev), k).wait_send())


    def s_left(s, unused):
        for dx in range(1, nx):
            for copy in x_copies(s, x, lax.rem(x + dx, nx), dx):
                copy.wait_send()
        for xo in range(nx):
            for copy in c_copies(s, xo, c, sz.at[s, 0]):
                copy.wait_send()
        return unused
    lax.fori_loop(0, nz, s_left, 0)


def solve_kernel(inv_root, all_ref, cent_ref, out_ref):
    tiles, size, wide = all_ref.shape
    walkers = tiles * size
    lane = lax.broadcasted_iota(jnp.int32, (size, walkers), 1)
    sub = lax.broadcasted_iota(jnp.int32, (size, walkers), 0)
    a = [all_ref[i, :, 0:walkers] for i in range(tiles)]
    e = [all_ref[i, :, walkers:wide] for i in range(tiles)]
    diagonal = [lane == sub + size * i for i in range(tiles)]
    picked = jnp.where(diagonal[0], a[0], 0.0)
    total = e[0]
    for i in range(1, tiles):
        picked = picked + jnp.where(diagonal[i], a[i], 0.0)
        total = total + e[i]
    shift = 0.01 * jnp.sum(jnp.sum(picked, axis=0, keepdims=True), axis=1, keepdims=True) / walkers
    average = jnp.sum(total, axis=0, keepdims=True) / walkers
    y = [(e[i] - average) * inv_root for i in range(tiles)]
    a = [a[i] + jnp.where(diagonal[i], shift, 0.0) for i in range(tiles)]

    for k in range(tiles):
        spread = [
            [jnp.broadcast_to(a[i][:, size * k + j:size * k + j + 1], (size, walkers)) for j in range(size)]
            for i in range(tiles)
        ]
        c = list(spread[k])
        row, right = a[k], y[k]
        scale = jnp.zeros((size, walkers), jnp.float32)
        for j in range(size):
            inverse = 1.0 / c[j][j:j + 1, :]
            factor = jnp.where(sub == j, 0.0, c[j]) * inverse
            for l in range(j + 1, size):
                c[l] = c[l] - factor * c[l][j:j + 1, :]
            row = row - factor * row[j:j + 1, :]
            right = right - factor * right[j:j + 1, :]
            scale = jnp.where(sub == j, inverse, scale)
        row, right = row * scale, right * scale
        a[k], y[k] = row, right
        order = [(k + 1 + i) % tiles for i in range(tiles - 1)]
        for i in order:
            for j in range(size):
                if k + 1 < tiles:
                    a[i] = a[i] - spread[i][j] * row[j:j + 1, :]
                y[i] = y[i] - spread[i][j] * right[j:j + 1, :]

    weights = [v.astype(jnp.bfloat16).astype(jnp.float32) for v in y]
    column = jnp.concatenate(weights, axis=0)
    rows, _, width = cent_ref.shape
    column = jnp.concatenate([column] * (width // walkers), axis=1)

    def project(r, unused):
        base = pl.multiple_of(r * 8, 8)
        parts = [
            jnp.sum(cent_ref[base + q].astype(jnp.float32) * column, axis=0, keepdims=True) for q in range(8)
        ]
        out_ref[pl.ds(base, 8), :] = jnp.concatenate(parts, axis=0)
        return unused
    lax.fori_loop(0, rows // 8, project, 0)


def body(nz, nx, layer_input, mixed_heads, cotangents, local_energy):
    nc = 2
    ndev = nz * nx * nc
    walk_dev, elec, width = layer_input.shape
    walkers = walk_dev * ndev
    inv_root = 1.0 / math.sqrt(walkers)
    rows = 4 * width // ndev
    rows_held = max(rows, 16)
    used = elec * walk_dev
    depth = -(-used // 128) * 128
    layer_rows = jnp.swapaxes(layer_input, 0, 1).reshape(used, width)
    heads_rows = jnp.swapaxes(mixed_heads, 0, 1).reshape(used, width)
    cots = jnp.transpose(cotangents, (1, 2, 0, 3)).reshape(4, used, width)

    bf, f32 = jnp.bfloat16, jnp.float32
    dma = pltpu.SemaphoreType.DMA
    vmem = pl.BlockSpec(memory_space=pltpu.VMEM)
    centered, everything = pl.pallas_call(
        functools.partial(gather_kernel, nz, nx, rows, inv_root),
        out_shape=(
            jax.ShapeDtypeStruct((rows, walkers, width), bf),
            jax.ShapeDtypeStruct((ndev, walk_dev, walkers + 128), f32),
        ),
        in_specs=[vmem] * 3 + [pl.BlockSpec(memory_space=pltpu.SMEM)],
        out_specs=(vmem, vmem),
        scratch_shapes=[
            pltpu.VMEM((ndev, rows_held, depth), bf),
            pltpu.VMEM((ndev, depth, width), bf),
            pltpu.VMEM((nz, nx * nc, rows_held, depth), bf),
            pltpu.VMEM((nx, nz, nc, rows_held, depth), bf),
            pltpu.VMEM((ndev, rows_held, depth), bf),
            pltpu.VMEM((rows, walkers, width), bf),
            pltpu.VMEM((ndev, walk_dev, walkers), f32),
            pltpu.VMEM((ndev, walk_dev, walkers), f32),
            pltpu.VMEM((ndev, walk_dev, walkers + 128), f32),
        ] + [dma((nz,))] * 2 + [dma((nx, nz))] * 10 + [dma((ndev,))] * 4,
        compiler_params=pltpu.CompilerParams(
            collective_id=0, has_side_effects=True, vmem_limit_bytes=(24 if ndev <= 16 else 56) << 20
        ),
        name="gather_gram",
    )(layer_rows, heads_rows, cots, local_energy)
    if walkers == 128:
        return pl.pallas_call(
            functools.partial(solve_kernel, inv_root),
            out_shape=jax.ShapeDtypeStruct((rows, width), f32),
            in_specs=[vmem] * 2,
            out_specs=vmem,
            compiler_params=pltpu.CompilerParams(vmem_limit_bytes=16 << 20),
            name="solve_project",
        )(everything, centered)
    everything = everything.reshape(walkers, walkers + 128)
    gram = everything[:, :walkers]
    energies = everything[:, walkers]
    right_side = (energies - jnp.mean(energies)) * inv_root
    damped = gram + 0.01 * jnp.trace(gram) / walkers * jnp.eye(walkers, dtype=f32)
    weights = solve_damped(damped, right_side).astype(bf)
    return jnp.einsum("w,rwj->rj", weights, centered, preferred_element_type=f32)


def solution(mesh):
    lanes = ("groups", "wide", "pair", "cores")
    placed = (
        P(lanes, None, None),
        P(lanes, None, None),
        P(lanes, None, None, None),
        P(lanes),
    )
    return jax.shard_map(
        functools.partial(body, mesh.shape["wide"], mesh.shape["pair"]),
        mesh=mesh,
        in_specs=placed,
        out_specs=P(lanes, None),
        check_vma=False,
    )
```

```python
import functools
import math

import jax
import jax.numpy as jnp
from jax import lax
from jax.experimental import pallas as pl
from jax.experimental.pallas import tpu as pltpu
from jax.sharding import PartitionSpec as P

MESH = pl.DeviceIdType.MESH
AXES = ("groups", "wide", "pair", "cores")


def solve_damped(damped, right_side):
    lower = jnp.linalg.cholesky(damped)
    forward = jax.scipy.linalg.solve_triangular(lower, right_side, lower=True)
    return jax.scipy.linalg.solve_triangular(lower, forward, lower=True, trans=1)


def gather_kernel(
    nz, nx, rows, inv_root,
    layer_ref, heads_ref, c_ref, en_ref, cent_ref, gall_ref,
    st_ref, cbuf, sz, sx, sbuf, grads, gpart, rbuf, gbuf,
    zs_c, zr_c, zs_s, zr_s, xs_c, xr_c, xs_s, xr_s, cs_c, cr_c, cs_s, cr_s,
    gs, gr, hs, hr,
):
    g, z, x, c = (lax.axis_index(a) for a in AXES)
    nc = 2
    ndev = nz * nx * nc
    sib = 1 - c
    me = (z * nx + x) * nc + c
    depth = cbuf.shape[1]
    width = cbuf.shape[2]
    walk = ndev * 8

    def dev(d):
        return (g, d // (nx * nc), (d // nc) % nx, d % nc)

    barrier = pltpu.get_barrier_semaphore()

    def greet(k, unused):
        d = lax.rem(me + k, ndev)
        pl.semaphore_signal(barrier, inc=1, device_id=dev(d), device_id_type=MESH)
        return unused
    lax.fori_loop(1, ndev, greet, 0, unroll=ndev <= 16)

    used = c_ref.shape[1]

    def clear(o, unused):
        cbuf[o, used:depth, :] = jnp.zeros((depth - used, width), cbuf.dtype)
        return unused
    lax.fori_loop(0, ndev, clear, 0)
    st_ref[...] = jnp.zeros_like(st_ref)
    slabs = width // rows
    for source, first_slab, times in ((layer_ref, 0, 3), (heads_ref, 3 * slabs, 1)):
        turned = source[...].astype(jnp.float32).T.astype(jnp.bfloat16).reshape(slabs, rows, used)
        for again in range(times):
            at = first_slab + again * slabs
            st_ref[at:at + slabs, 0:rows, 0:used] = turned
    pl.semaphore_wait(barrier, ndev - 1)

    def origin(s, xx, cc):
        return (s * nx + xx) * nc + cc

    def z_copies(zt, src_z, dz):
        m = (4 * zt) // nz
        o = origin(src_z, x, c)
        copies = [pltpu.make_async_remote_copy(
            c_ref.at[m], cbuf.at[o, pl.ds(0, used)], zs_c.at[dz], zr_c.at[src_z],
            device_id=(g, zt, x, c), device_id_type=MESH)]
        for dx in range(1, nx + 1):
            xt = lax.rem(x + dx, nx)
            copies.append(pltpu.make_async_remote_copy(
                st_ref.at[pl.ds((zt * nx + xt) * nc, nc)], sz.at[src_z, pl.ds(xt * nc, nc)],
                zs_s.at[dx - 1, dz], zr_s.at[dx - 1, src_z],
                device_id=(g, zt, x, c), device_id_type=MESH))
        return copies

    def x_copies(s, xo, xt, dx):
        o = origin(s, xo, c)
        return (
            pltpu.make_async_remote_copy(
                cbuf.at[o, pl.ds(0, used)], cbuf.at[o, pl.ds(0, used)], xs_c.at[dx, s], xr_c.at[xo, s],
                device_id=(g, z, xt, c), device_id_type=MESH),
            pltpu.make_async_remote_copy(
                sz.at[s, pl.ds(xt * nc, nc)], sx.at[xo, s], xs_s.at[dx, s], xr_s.at[xo, s],
                device_id=(g, z, xt, c), device_id_type=MESH),
        )

    def c_copies(s, xo, co, src):
        o = origin(s, xo, co)
        return (
            pltpu.make_async_remote_copy(
                cbuf.at[o, pl.ds(0, used)], cbuf.at[o, pl.ds(0, used)], cs_c.at[xo, s], cr_c.at[xo, s],
                device_id=(g, z, x, sib), device_id_type=MESH),
            pltpu.make_async_remote_copy(
                src, sbuf.at[o], cs_s.at[xo, s], cr_s.at[xo, s],
                device_id=(g, z, x, sib), device_id_type=MESH),
        )

    half = nz // 2

    def offset(t):
        away = jnp.where(lax.rem(t, 2) == 0, half - t // 2, half + t // 2)
        return jnp.where(t == 0, 0, away)

    def z_round(t):
        return z_copies(lax.rem(z + offset(t), nz), z, t)

    def z_from(t):
        return lax.rem(z + nz - offset(t), nz)

    for copy in z_round(1) + z_round(2)[:1]:
        copy.start()

    cbuf[me, 0:used, :] = c_ref[(4 * z) // nz]
    sz[z] = st_ref[pl.ds(z * nx * nc, nx * nc)]

    slot = lax.broadcasted_iota(jnp.int32, (8, depth), 1)
    walker = lax.broadcasted_iota(jnp.int32, (8, depth), 0)
    own = lax.rem(slot, 8) == walker
    step = min(rows, 16)

    def form(p):
        def part(k, unused):
            base = pl.multiple_of(k * step, step)
            halves = []
            for h in range(nc):
                piece = sbuf[p * nc + h, pl.ds(base, step), :].astype(jnp.float32)
                spread = jnp.where(own[None], piece[:, None, :], 0.0)
                left = spread.reshape(step * 8, depth).astype(jnp.bfloat16)
                out = jnp.dot(left, cbuf[p * nc + h], preferred_element_type=jnp.float32)
                halves.append(out.reshape(step, 8, width))
            both = jnp.concatenate(halves, axis=1).astype(jnp.bfloat16)
            grads[pl.ds(base, step), pl.ds(pl.multiple_of(p * 16, 16), 16), :] = both
            return unused
        lax.fori_loop(0, rows // step, part, 0)

    def pipeline(t, unused):
        @pl.when(t >= 2)
        def third():
            s = z_from(t - 2)
            for dx in range(nx):
                xo = lax.rem(x + nx - dx, nx)
                for copy in c_copies(s, xo, sib, sz.at[s, 0]):
                    copy.wait_recv()
                form(s * nx + xo)

        @pl.when(t < nz)
        def first():
            s = z_from(t)

            def land(j):
                @pl.when(t > 0)
                def arrived():
                    z_round(t)[j].wait_send()
                    ahead = 1 if j < nx else 2

                    @pl.when(t + ahead < nz)
                    def onward():
                        z_round(t + ahead)[(j + 1) % (nx + 1)].start()
                    z_copies(z, s, 0)[j].wait_recv()

            to_sib = c_copies(s, x, c, sz.at[s, x * nc + sib])
            land(0)
            for dx in range(1, nx):
                x_copies(s, x, lax.rem(x + dx, nx), dx)[0].start()
            to_sib[0].start()
            for dx in range(1, nx):
                land(dx)
                x_copies(s, x, lax.rem(x + dx, nx), dx)[1].start()
            land(nx)
            to_sib[1].start()
            sbuf[origin(s, x, c)] = sz[s, x * nc + c]

        @pl.when((t >= 1) & (t < nz + 1))
        def second():
            s = z_from(t - 1)
            for dx in range(1, nx):
                xo = lax.rem(x + nx - dx, nx)
                for copy, onward in zip(x_copies(s, xo, x, 0), c_copies(s, xo, c, sx.at[xo, s, sib])):
                    copy.wait_recv()
                    onward.start()
                sbuf[origin(s, xo, c)] = sx[xo, s, c]
        return unused
    lax.fori_loop(0, nz + 2, pipeline, 0)

    gpart[...] = jnp.zeros_like(gpart)
    batch = 4

    def share(k, unused):
        pieces = []
        for j in range(batch):
            stored = grads[k * batch + j].astype(jnp.float32)
            average = jnp.mean(stored, axis=0, keepdims=True)
            piece = ((stored - average) * inv_root).astype(jnp.bfloat16)
            cent_ref[k * batch + j] = piece
            pieces.append(piece)
        flat = jnp.concatenate(pieces, axis=1)
        for r in range(walk // 128):
            add = lax.dot_general(flat[r * 128:(r + 1) * 128], flat, (((1,), (1,)), ((), ())),
                                  preferred_element_type=jnp.float32)
            gpart[r * 16:(r + 1) * 16] += add.reshape(16, 8, walk)
        return unused
    lax.fori_loop(0, rows // batch, share, 0, unroll=4 if ndev <= 16 else 1)

    def g_copy(src_d, dst_d, k):
        return pltpu.make_async_remote_copy(
            gpart.at[dst_d], rbuf.at[src_d], gs.at[k], gr.at[src_d], device_id=dev(dst_d), device_id_type=MESH)

    def h_copy(src_d, dst_d, k):
        return pltpu.make_async_remote_copy(
            gbuf.at[src_d], gbuf.at[src_d], hs.at[k], hr.at[src_d], device_id=dev(dst_d), device_id_type=MESH)

    def each(fn):
        def run(k, unused):
            fn(k)
            return unused
        lax.fori_loop(1, ndev, run, 0, unroll=ndev <= 16)

    each(lambda k: g_copy(me, lax.rem(me + k, ndev), k).start())
    rbuf[me] = gpart[me]
    each(lambda k: g_copy(lax.rem(me + k, ndev), me, k).wait_recv())
    gbuf[me, :, 0:walk] = jnp.sum(rbuf[...], axis=0)
    energy = jnp.zeros((8, 128), jnp.float32)
    place = lax.broadcasted_iota(jnp.int32, (8, 128), 0)
    for w in range(8):
        energy = jnp.where(place == w, en_ref[w], energy)
    gbuf[me, :, walk:walk + 128] = energy
    each(lambda k: h_copy(me, lax.rem(me + k, ndev), k).start())
    each(lambda k: h_copy(lax.rem(me + k, ndev), me, k).wait_recv())
    gall_ref[...] = gbuf[...]

    each(lambda k: g_copy(me, lax.rem(me + k, ndev), k).wait_send())
    each(lambda k: h_copy(me, lax.rem(me + k, ndev), k).wait_send())


    def s_left(s, unused):
        for dx in range(1, nx):
            for copy in x_copies(s, x, lax.rem(x + dx, nx), dx):
                copy.wait_send()
        for xo in range(nx):
            for copy in c_copies(s, xo, c, sz.at[s, 0]):
                copy.wait_send()
        return unused
    lax.fori_loop(0, nz, s_left, 0)


def solve_kernel(inv_root, all_ref, cent_ref, out_ref):
    tiles, size, wide = all_ref.shape
    walkers = tiles * size
    lane = lax.broadcasted_iota(jnp.int32, (size, walkers), 1)
    sub = lax.broadcasted_iota(jnp.int32, (size, walkers), 0)
    a = [all_ref[i, :, 0:walkers] for i in range(tiles)]
    e = [all_ref[i, :, walkers:wide] for i in range(tiles)]
    diagonal = [lane == sub + size * i for i in range(tiles)]
    picked = jnp.where(diagonal[0], a[0], 0.0)
    total = e[0]
    for i in range(1, tiles):
        picked = picked + jnp.where(diagonal[i], a[i], 0.0)
        total = total + e[i]
    shift = 0.01 * jnp.sum(jnp.sum(picked, axis=0, keepdims=True), axis=1, keepdims=True) / walkers
    average = jnp.sum(total, axis=0, keepdims=True) / walkers
    y = [(e[i] - average) * inv_root for i in range(tiles)]
    a = [a[i] + jnp.where(diagonal[i], shift, 0.0) for i in range(tiles)]

    for k in range(tiles):
        spread = [
            [jnp.broadcast_to(a[i][:, size * k + j:size * k + j + 1], (size, walkers)) for j in range(size)]
            for i in range(tiles)
        ]
        c = list(spread[k])
        row, right = a[k], y[k]
        scale = jnp.zeros((size, walkers), jnp.float32)
        for j in range(size):
            inverse = 1.0 / c[j][j:j + 1, :]
            factor = jnp.where(sub == j, 0.0, c[j]) * inverse
            for l in range(j + 1, size):
                c[l] = c[l] - factor * c[l][j:j + 1, :]
            row = row - factor * row[j:j + 1, :]
            right = right - factor * right[j:j + 1, :]
            scale = jnp.where(sub == j, inverse, scale)
        row, right = row * scale, right * scale
        a[k], y[k] = row, right
        order = [(k + 1 + i) % tiles for i in range(tiles - 1)]
        for i in order:
            for j in range(size):
                a[i] = a[i] - spread[i][j] * row[j:j + 1, :]
                if k == 0:
                    y[i] = y[i] - spread[i][j] * right[j:j + 1, :]
        if k == 0:
            a = [jnp.where(lane == 0, y[i], a[i]) for i in range(tiles)]
    y = [jnp.broadcast_to(a[i][:, 0:1], (size, walkers)) for i in range(tiles)]

    weights = [v.astype(jnp.bfloat16).astype(jnp.float32) for v in y]
    column = jnp.concatenate(weights, axis=0)
    rows, _, width = cent_ref.shape
    column = jnp.concatenate([column] * (width // walkers), axis=1)

    def project(r, unused):
        base = pl.multiple_of(r * 8, 8)
        parts = [
            jnp.sum(cent_ref[base + q].astype(jnp.float32) * column, axis=0, keepdims=True) for q in range(8)
        ]
        out_ref[pl.ds(base, 8), :] = jnp.concatenate(parts, axis=0)
        return unused
    lax.fori_loop(0, rows // 8, project, 0)


def body(nz, nx, layer_input, mixed_heads, cotangents, local_energy):
    nc = 2
    ndev = nz * nx * nc
    walk_dev, elec, width = layer_input.shape
    walkers = walk_dev * ndev
    inv_root = 1.0 / math.sqrt(walkers)
    rows = 4 * width // ndev
    rows_held = max(rows, 16)
    used = elec * walk_dev
    depth = -(-used // 128) * 128
    layer_rows = jnp.swapaxes(layer_input, 0, 1).reshape(used, width)
    heads_rows = jnp.swapaxes(mixed_heads, 0, 1).reshape(used, width)
    cots = jnp.transpose(cotangents, (1, 2, 0, 3)).reshape(4, used, width)

    bf, f32 = jnp.bfloat16, jnp.float32
    dma = pltpu.SemaphoreType.DMA
    vmem = pl.BlockSpec(memory_space=pltpu.VMEM)
    centered, everything = pl.pallas_call(
        functools.partial(gather_kernel, nz, nx, rows, inv_root),
        out_shape=(
            jax.ShapeDtypeStruct((rows, walkers, width), bf),
            jax.ShapeDtypeStruct((ndev, walk_dev, walkers + 128), f32),
        ),
        in_specs=[vmem] * 3 + [pl.BlockSpec(memory_space=pltpu.SMEM)],
        out_specs=(vmem, vmem),
        scratch_shapes=[
            pltpu.VMEM((ndev, rows_held, depth), bf),
            pltpu.VMEM((ndev, depth, width), bf),
            pltpu.VMEM((nz, nx * nc, rows_held, depth), bf),
            pltpu.VMEM((nx, nz, nc, rows_held, depth), bf),
            pltpu.VMEM((ndev, rows_held, depth), bf),
            pltpu.VMEM((rows, walkers, width), bf),
            pltpu.VMEM((ndev, walk_dev, walkers), f32),
            pltpu.VMEM((ndev, walk_dev, walkers), f32),
            pltpu.VMEM((ndev, walk_dev, walkers + 128), f32),
        ] + [dma((nz,))] * 2 + [dma((nx, nz))] * 10 + [dma((ndev,))] * 4,
        compiler_params=pltpu.CompilerParams(
            collective_id=0, has_side_effects=True, vmem_limit_bytes=(24 if ndev <= 16 else 56) << 20
        ),
        name="gather_gram",
    )(layer_rows, heads_rows, cots, local_energy)
    if walkers == 128:
        return pl.pallas_call(
            functools.partial(solve_kernel, inv_root),
            out_shape=jax.ShapeDtypeStruct((rows, width), f32),
            in_specs=[vmem] * 2,
            out_specs=vmem,
            compiler_params=pltpu.CompilerParams(vmem_limit_bytes=16 << 20),
            name="solve_project",
        )(everything, centered)
    everything = everything.reshape(walkers, walkers + 128)
    gram = everything[:, :walkers]
    energies = everything[:, walkers]
    right_side = (energies - jnp.mean(energies)) * inv_root
    damped = gram + 0.01 * jnp.trace(gram) / walkers * jnp.eye(walkers, dtype=f32)
    weights = solve_damped(damped, right_side).astype(bf)
    return jnp.einsum("w,rwj->rj", weights, centered, preferred_element_type=f32)


def solution(mesh):
    lanes = ("groups", "wide", "pair", "cores")
    placed = (
        P(lanes, None, None),
        P(lanes, None, None),
        P(lanes, None, None, None),
        P(lanes),
    )
    return jax.shard_map(
        functools.partial(body, mesh.shape["wide"], mesh.shape["pair"]),
        mesh=mesh,
        in_specs=placed,
        out_specs=P(lanes, None),
        check_vma=False,
    )
```

```python
import functools
import math

import jax
import jax.numpy as jnp
from jax import lax
from jax.experimental import pallas as pl
from jax.experimental.pallas import tpu as pltpu
from jax.sharding import PartitionSpec as P

MESH = pl.DeviceIdType.MESH
AXES = ("groups", "wide", "pair", "cores")


def solve_damped(damped, right_side):
    lower = jnp.linalg.cholesky(damped)
    forward = jax.scipy.linalg.solve_triangular(lower, right_side, lower=True)
    return jax.scipy.linalg.solve_triangular(lower, forward, lower=True, trans=1)


def gather_kernel(
    nz, nx, rows, inv_root,
    layer_ref, heads_ref, c_ref, en_ref, cent_ref, gall_ref,
    st_ref, cbuf, sz, sx, sbuf, grads, gpart, rbuf, gbuf,
    zs_c, zr_c, zs_s, zr_s, xs_c, xr_c, xs_s, xr_s, cs_c, cr_c, cs_s, cr_s,
    gs, gr, hs, hr,
):
    g, z, x, c = (lax.axis_index(a) for a in AXES)
    nc = 2
    ndev = nz * nx * nc
    sib = 1 - c
    me = (z * nx + x) * nc + c
    depth = cbuf.shape[1]
    width = cbuf.shape[2]
    walk = ndev * 8

    def dev(d):
        return (g, d // (nx * nc), (d // nc) % nx, d % nc)

    barrier = pltpu.get_barrier_semaphore()

    def greet(k, unused):
        d = lax.rem(me + k, ndev)
        pl.semaphore_signal(barrier, inc=1, device_id=dev(d), device_id_type=MESH)
        return unused
    lax.fori_loop(1, ndev, greet, 0, unroll=ndev <= 16)

    used = c_ref.shape[1]

    def clear(o, unused):
        cbuf[o, used:depth, :] = jnp.zeros((depth - used, width), cbuf.dtype)
        return unused
    lax.fori_loop(0, ndev, clear, 0)
    st_ref[...] = jnp.zeros_like(st_ref)
    slabs = width // rows
    for source, first_slab, times in ((layer_ref, 0, 3), (heads_ref, 3 * slabs, 1)):
        turned = source[...].astype(jnp.float32).T.astype(jnp.bfloat16).reshape(slabs, rows, used)
        for again in range(times):
            at = first_slab + again * slabs
            st_ref[at:at + slabs, 0:rows, 0:used] = turned
    pl.semaphore_wait(barrier, ndev - 1)

    def origin(s, xx, cc):
        return (s * nx + xx) * nc + cc

    def z_copies(zt, src_z, dz):
        m = (4 * zt) // nz
        o = origin(src_z, x, c)
        copies = [pltpu.make_async_remote_copy(
            c_ref.at[m], cbuf.at[o, pl.ds(0, used)], zs_c.at[dz], zr_c.at[src_z],
            device_id=(g, zt, x, c), device_id_type=MESH)]
        for dx in range(1, nx + 1):
            xt = lax.rem(x + dx, nx)
            copies.append(pltpu.make_async_remote_copy(
                st_ref.at[pl.ds((zt * nx + xt) * nc, nc)], sz.at[src_z, pl.ds(xt * nc, nc)],
                zs_s.at[dx - 1, dz], zr_s.at[dx - 1, src_z],
                device_id=(g, zt, x, c), device_id_type=MESH))
        return copies

    def x_copies(s, xo, xt, dx):
        o = origin(s, xo, c)
        return (
            pltpu.make_async_remote_copy(
                cbuf.at[o, pl.ds(0, used)], cbuf.at[o, pl.ds(0, used)], xs_c.at[dx, s], xr_c.at[xo, s],
                device_id=(g, z, xt, c), device_id_type=MESH),
            pltpu.make_async_remote_copy(
                sz.at[s, pl.ds(xt * nc, nc)], sx.at[xo, s], xs_s.at[dx, s], xr_s.at[xo, s],
                device_id=(g, z, xt, c), device_id_type=MESH),
        )

    def c_copies(s, xo, co, src):
        o = origin(s, xo, co)
        return (
            pltpu.make_async_remote_copy(
                cbuf.at[o, pl.ds(0, used)], cbuf.at[o, pl.ds(0, used)], cs_c.at[xo, s], cr_c.at[xo, s],
                device_id=(g, z, x, sib), device_id_type=MESH),
            pltpu.make_async_remote_copy(
                src, sbuf.at[o], cs_s.at[xo, s], cr_s.at[xo, s],
                device_id=(g, z, x, sib), device_id_type=MESH),
        )

    half = nz // 2

    def offset(t):
        away = jnp.where(lax.rem(t, 2) == 0, half - t // 2, half + t // 2)
        return jnp.where(t == 0, 0, away)

    def z_round(t):
        return z_copies(lax.rem(z + offset(t), nz), z, t)

    def z_from(t):
        return lax.rem(z + nz - offset(t), nz)

    for copy in z_round(1) + z_round(2)[:1]:
        copy.start()

    cbuf[me, 0:used, :] = c_ref[(4 * z) // nz]
    sz[z] = st_ref[pl.ds(z * nx * nc, nx * nc)]

    slot = lax.broadcasted_iota(jnp.int32, (8, depth), 1)
    walker = lax.broadcasted_iota(jnp.int32, (8, depth), 0)
    own = lax.rem(slot, 8) == walker
    step = min(rows, 16)

    def form(p):
        def part(k, unused):
            base = pl.multiple_of(k * step, step)
            halves = []
            for h in range(nc):
                piece = sbuf[p * nc + h, pl.ds(base, step), :].astype(jnp.float32)
                spread = jnp.where(own[None], piece[:, None, :], 0.0)
                left = spread.reshape(step * 8, depth).astype(jnp.bfloat16)
                out = jnp.dot(left, cbuf[p * nc + h], preferred_element_type=jnp.float32)
                halves.append(out.reshape(step, 8, width))
            both = jnp.concatenate(halves, axis=1).astype(jnp.bfloat16)
            grads[pl.ds(base, step), pl.ds(pl.multiple_of(p * 16, 16), 16), :] = both
            return unused
        lax.fori_loop(0, rows // step, part, 0, unroll=True)

    def pipeline(t, unused):
        @pl.when(t >= 2)
        def third():
            s = z_from(t - 2)
            for dx in range(nx):
                xo = lax.rem(x + nx - dx, nx)
                for copy in c_copies(s, xo, sib, sz.at[s, 0]):
                    copy.wait_recv()
                form(s * nx + xo)

        @pl.when(t < nz)
        def first():
            s = z_from(t)

            def land(j):
                @pl.when(t > 0)
                def arrived():
                    z_round(t)[j].wait_send()
                    ahead = 1 if j < nx else 2

                    @pl.when(t + ahead < nz)
                    def onward():
                        z_round(t + ahead)[(j + 1) % (nx + 1)].start()
                    z_copies(z, s, 0)[j].wait_recv()

            to_sib = c_copies(s, x, c, sz.at[s, x * nc + sib])
            land(0)
            for dx in range(1, nx):
                x_copies(s, x, lax.rem(x + dx, nx), dx)[0].start()
            to_sib[0].start()
            for dx in range(1, nx):
                land(dx)
                x_copies(s, x, lax.rem(x + dx, nx), dx)[1].start()
            land(nx)
            to_sib[1].start()
            sbuf[origin(s, x, c)] = sz[s, x * nc + c]

        @pl.when((t >= 1) & (t < nz + 1))
        def second():
            s = z_from(t - 1)
            for dx in range(1, nx):
                xo = lax.rem(x + nx - dx, nx)
                for copy, onward in zip(x_copies(s, xo, x, 0), c_copies(s, xo, c, sx.at[xo, s, sib])):
                    copy.wait_recv()
                    onward.start()
                sbuf[origin(s, xo, c)] = sx[xo, s, c]
        return unused
    lax.fori_loop(0, nz + 2, pipeline, 0)

    gpart[...] = jnp.zeros_like(gpart)
    batch = 4

    def share(k, unused):
        pieces = []
        for j in range(batch):
            stored = grads[k * batch + j].astype(jnp.float32)
            average = jnp.mean(stored, axis=0, keepdims=True)
            piece = ((stored - average) * inv_root).astype(jnp.bfloat16)
            cent_ref[k * batch + j] = piece
            pieces.append(piece)
        flat = jnp.concatenate(pieces, axis=1)
        for r in range(walk // 128):
            add = lax.dot_general(flat[r * 128:(r + 1) * 128], flat, (((1,), (1,)), ((), ())),
                                  preferred_element_type=jnp.float32)
            gpart[r * 16:(r + 1) * 16] += add.reshape(16, 8, walk)
        return unused
    lax.fori_loop(0, rows // batch, share, 0, unroll=4 if ndev <= 16 else 1)

    def g_copy(src_d, dst_d, k):
        return pltpu.make_async_remote_copy(
            gpart.at[dst_d], rbuf.at[src_d], gs.at[k], gr.at[src_d], device_id=dev(dst_d), device_id_type=MESH)

    def h_copy(src_d, dst_d, k):
        return pltpu.make_async_remote_copy(
            gbuf.at[src_d], gbuf.at[src_d], hs.at[k], hr.at[src_d], device_id=dev(dst_d), device_id_type=MESH)

    def each(fn):
        def run(k, unused):
            fn(k)
            return unused
        lax.fori_loop(1, ndev, run, 0, unroll=ndev <= 16)

    each(lambda k: g_copy(me, lax.rem(me + k, ndev), k).start())
    rbuf[me] = gpart[me]
    each(lambda k: g_copy(lax.rem(me + k, ndev), me, k).wait_recv())
    gbuf[me, :, 0:walk] = jnp.sum(rbuf[...], axis=0)
    energy = jnp.zeros((8, 128), jnp.float32)
    place = lax.broadcasted_iota(jnp.int32, (8, 128), 0)
    for w in range(8):
        energy = jnp.where(place == w, en_ref[w], energy)
    gbuf[me, :, walk:walk + 128] = energy
    each(lambda k: h_copy(me, lax.rem(me + k, ndev), k).start())
    each(lambda k: h_copy(lax.rem(me + k, ndev), me, k).wait_recv())
    gall_ref[...] = gbuf[...]

    each(lambda k: g_copy(me, lax.rem(me + k, ndev), k).wait_send())
    each(lambda k: h_copy(me, lax.rem(me + k, ndev), k).wait_send())


    def s_left(s, unused):
        for dx in range(1, nx):
            for copy in x_copies(s, x, lax.rem(x + dx, nx), dx):
                copy.wait_send()
        for xo in range(nx):
            for copy in c_copies(s, xo, c, sz.at[s, 0]):
                copy.wait_send()
        return unused
    lax.fori_loop(0, nz, s_left, 0)


def solve_kernel(inv_root, all_ref, cent_ref, out_ref):
    tiles, size, wide = all_ref.shape
    walkers = tiles * size
    lane = lax.broadcasted_iota(jnp.int32, (size, walkers), 1)
    sub = lax.broadcasted_iota(jnp.int32, (size, walkers), 0)
    a = [all_ref[i, :, 0:walkers] for i in range(tiles)]
    e = [all_ref[i, :, walkers:wide] for i in range(tiles)]
    diagonal = [lane == sub + size * i for i in range(tiles)]
    picked = jnp.where(diagonal[0], a[0], 0.0)
    total = e[0]
    for i in range(1, tiles):
        picked = picked + jnp.where(diagonal[i], a[i], 0.0)
        total = total + e[i]
    shift = 0.01 * jnp.sum(jnp.sum(picked, axis=0, keepdims=True), axis=1, keepdims=True) / walkers
    average = jnp.sum(total, axis=0, keepdims=True) / walkers
    y = [(e[i] - average) * inv_root for i in range(tiles)]
    a = [a[i] + jnp.where(diagonal[i], shift, 0.0) for i in range(tiles)]

    for k in range(tiles):
        spread = [
            [jnp.broadcast_to(a[i][:, size * k + j:size * k + j + 1], (size, walkers)) for j in range(size)]
            for i in range(tiles)
        ]
        c = list(spread[k])
        row, right = a[k], y[k]
        scale = jnp.zeros((size, walkers), jnp.float32)
        for j in range(size):
            inverse = 1.0 / c[j][j:j + 1, :]
            factor = jnp.where(sub == j, 0.0, c[j]) * inverse
            for l in range(j + 1, size):
                c[l] = c[l] - factor * c[l][j:j + 1, :]
            row = row - factor * row[j:j + 1, :]
            right = right - factor * right[j:j + 1, :]
            scale = jnp.where(sub == j, inverse, scale)
        row, right = row * scale, right * scale
        a[k], y[k] = row, right
        order = [(k + 1 + i) % tiles for i in range(tiles - 1)]
        for i in order:
            for j in range(size):
                a[i] = a[i] - spread[i][j] * row[j:j + 1, :]
                if k == 0:
                    y[i] = y[i] - spread[i][j] * right[j:j + 1, :]
        if k == 0:
            a = [jnp.where(lane == 0, y[i], a[i]) for i in range(tiles)]
    y = [jnp.broadcast_to(a[i][:, 0:1], (size, walkers)) for i in range(tiles)]

    weights = [v.astype(jnp.bfloat16).astype(jnp.float32) for v in y]
    column = jnp.concatenate(weights, axis=0)
    rows, _, width = cent_ref.shape
    column = jnp.concatenate([column] * (width // walkers), axis=1)

    def project(r, unused):
        base = pl.multiple_of(r * 8, 8)
        parts = [
            jnp.sum(cent_ref[base + q].astype(jnp.float32) * column, axis=0, keepdims=True) for q in range(8)
        ]
        out_ref[pl.ds(base, 8), :] = jnp.concatenate(parts, axis=0)
        return unused
    lax.fori_loop(0, rows // 8, project, 0)


def body(nz, nx, layer_input, mixed_heads, cotangents, local_energy):
    nc = 2
    ndev = nz * nx * nc
    walk_dev, elec, width = layer_input.shape
    walkers = walk_dev * ndev
    inv_root = 1.0 / math.sqrt(walkers)
    rows = 4 * width // ndev
    rows_held = max(rows, 16)
    used = elec * walk_dev
    depth = -(-used // 128) * 128
    layer_rows = jnp.swapaxes(layer_input, 0, 1).reshape(used, width)
    heads_rows = jnp.swapaxes(mixed_heads, 0, 1).reshape(used, width)
    cots = jnp.transpose(cotangents, (1, 2, 0, 3)).reshape(4, used, width)

    bf, f32 = jnp.bfloat16, jnp.float32
    dma = pltpu.SemaphoreType.DMA
    vmem = pl.BlockSpec(memory_space=pltpu.VMEM)
    centered, everything = pl.pallas_call(
        functools.partial(gather_kernel, nz, nx, rows, inv_root),
        out_shape=(
            jax.ShapeDtypeStruct((rows, walkers, width), bf),
            jax.ShapeDtypeStruct((ndev, walk_dev, walkers + 128), f32),
        ),
        in_specs=[vmem] * 3 + [pl.BlockSpec(memory_space=pltpu.SMEM)],
        out_specs=(vmem, vmem),
        scratch_shapes=[
            pltpu.VMEM((ndev, rows_held, depth), bf),
            pltpu.VMEM((ndev, depth, width), bf),
            pltpu.VMEM((nz, nx * nc, rows_held, depth), bf),
            pltpu.VMEM((nx, nz, nc, rows_held, depth), bf),
            pltpu.VMEM((ndev, rows_held, depth), bf),
            pltpu.VMEM((rows, walkers, width), bf),
            pltpu.VMEM((ndev, walk_dev, walkers), f32),
            pltpu.VMEM((ndev, walk_dev, walkers), f32),
            pltpu.VMEM((ndev, walk_dev, walkers + 128), f32),
        ] + [dma((nz,))] * 2 + [dma((nx, nz))] * 10 + [dma((ndev,))] * 4,
        compiler_params=pltpu.CompilerParams(
            collective_id=0, has_side_effects=True, vmem_limit_bytes=(24 if ndev <= 16 else 56) << 20
        ),
        name="gather_gram",
    )(layer_rows, heads_rows, cots, local_energy)
    if walkers == 128:
        return pl.pallas_call(
            functools.partial(solve_kernel, inv_root),
            out_shape=jax.ShapeDtypeStruct((rows, width), f32),
            in_specs=[vmem] * 2,
            out_specs=vmem,
            compiler_params=pltpu.CompilerParams(vmem_limit_bytes=16 << 20),
            name="solve_project",
        )(everything, centered)
    everything = everything.reshape(walkers, walkers + 128)
    gram = everything[:, :walkers]
    energies = everything[:, walkers]
    right_side = (energies - jnp.mean(energies)) * inv_root
    damped = gram + 0.01 * jnp.trace(gram) / walkers * jnp.eye(walkers, dtype=f32)
    weights = solve_damped(damped, right_side).astype(bf)
    return jnp.einsum("w,rwj->rj", weights, centered, preferred_element_type=f32)


def solution(mesh):
    lanes = ("groups", "wide", "pair", "cores")
    placed = (
        P(lanes, None, None),
        P(lanes, None, None),
        P(lanes, None, None, None),
        P(lanes),
    )
    return jax.shard_map(
        functools.partial(body, mesh.shape["wide"], mesh.shape["pair"]),
        mesh=mesh,
        in_specs=placed,
        out_specs=P(lanes, None),
        check_vma=False,
    )
```
